256 devices in a mesh: grp: 8 (over x, y_hi), exp: 32 (over z, y_lo, core).
Axes of the slice: x: 4, y: 4 (y_hi: 2, y_lo: 2; y = y_hi * 2 + y_lo), z: 8, core: 2. Of those that a mesh axis runs over, the one named last changes fastest.
Arguments:
- hidden: bfloat16 [8, 4096, 4096], P('grp', 'exp'), may hold values from -6 to 6
- queries: bfloat16 [8, 4096, 4096], P('grp', 'exp'), may hold values from -100 to 100
- response_key_value: bfloat16 [8, 4096, 512], P('grp', 'exp'), may hold values from -6 to 6
- prompt_kv: bfloat16 [8, 384, 512], P('grp', 'exp'), may hold values from -4 to 4
- lengths: int32 [8, 16], P('grp'), may hold values from 1 to 256, 3072 in all within a row
- out_weight: bfloat16 [4096, 4096], P('grp', 'exp'), may hold values from -0.09375 to 0.09375
- norm_gain: float32 [4096], replicated, may hold values from 0.5 to 1.5
- router: bfloat16 [4096, 128], replicated, may hold values from -0.078125 to 0.078125
- gate_up: bfloat16 [256, 4096, 768], P(('grp', 'exp')), may hold values from -0.09375 to 0.09375
- routes: int32 [8, 4096, 4], P('grp', 'exp'), may hold values from 0 to 127, all different within a row; in each aligned block of 128 rows (0 to 127, 128 to 255, ..., all dimensions but the last counted through in order) at most 6 rows name the same one
Outputs:
- resid_out: bfloat16 [8, 4096, 4096], P('grp', 'exp')
- expert_act: bfloat16 [256, 256, 6, 384], P(('grp', 'exp'))
The draws below stay inside these ranges and needn't reach their ends.
Inputs may be any that keep to these rules, and one draw needn't show every extreme that they name: `routes`: each row names 4 different experts; every expert is named somewhere. Among the pairs of one device's 128 rows no expert is named more than 6 times, and on some device some expert is named exactly 6 times.
All inputs are finite; a program needn't handle non-finite values.
Results may differ from the reference program's by a relative error of at most 0.018.
Values may be sent and summed in bfloat16 or wider, within the bound.
A program may use at most 128 MiB of HBM per device.

```python
import math
import jax
import jax.numpy as jnp
import numpy as np
from jax import lax

D = 4096
QUERY_HEADS = 32
KEY_VALUE_HEADS = 2
HEAD_SIZE = 128
FF = 768
ROUTES = 4
TOK_DEV = 128
FFH = 384
EXPERTS = 128
SLICES = 256
SOURCES = 256
CAP = 6
RESPONSE_LENGTH = 256
GROUP_RESPONSES = 16
RESPONSE_ROWS = 4096
PROMPT_LENGTH = 384
N_GRP = 8


def prompt_block(key):
    return jax.random.truncated_normal(key, -4.0, 4.0, (N_GRP, PROMPT_LENGTH, 2 * KEY_VALUE_HEADS * HEAD_SIZE), jnp.float32)


def draw_prompt_kv(key, part):
    values = prompt_block(key)
    return values.astype(jnp.bfloat16)


def draw_queries(key, part):
    key = jax.random.fold_in(key, 7)
    noise_key = jax.random.fold_in(key, 0)
    values = jax.random.truncated_normal(noise_key, -6.0, 6.0, (N_GRP, RESPONSE_ROWS, QUERY_HEADS * HEAD_SIZE), jnp.float32)
    return values.astype(jnp.bfloat16)


def levels(key, dims, shards, low, largest):
    level, own = 1.0, jax.random.fold_in(key, 6)
    for axis_at, blocks in shards:
        steps = jnp.exp(jax.random.uniform(jax.random.fold_in(own, axis_at), (blocks,), jnp.float32, low / len(shards), largest / len(shards)))
        level = level * jnp.repeat(steps, dims[axis_at] // blocks).reshape([-1 if axis == axis_at else 1 for axis in range(len(dims))])
    return level


def split_up(amount, total, limit, lean):
    loads = [(1 << 20) // math.isqrt(standing ** lean) + 1 for standing in range(2, amount + 1)]
    rest, given = total - limit - (amount - 1), [1] * (amount - 1)
    while rest > 0:
        candidates = [i for i in range(amount - 1) if given[i] < limit]
        mass, budget = sum([loads[i] for i in candidates]), rest
        for i in candidates:
            addition = min(limit - given[i], max(1, budget * loads[i] // mass), rest)
            given[i] = given[i] + addition
            rest = rest - addition
    return np.array([limit] + given)


def ragged_sizes(own_key, amount, total, reach, skew):
    if amount == 2:
        one = jax.random.randint(own_key, (), max(1, total - reach), min(reach, total - 1) + 1)
        return jnp.stack([one, total - one])
    sizes = jnp.asarray(split_up(amount, total, reach, skew), jnp.int32)
    twos = (amount - 1) // 2
    source_of, receiver = sizes[1:1 + 2 * twos:2], sizes[2:2 + 2 * twos:2]
    margin = jnp.minimum(source_of - 1, reach - receiver)
    moved = jax.random.randint(jax.random.fold_in(own_key, 1), (twos,), 0, 1 << 20) % (margin + 1)
    sizes = sizes.at[1:1 + 2 * twos:2].set(source_of - moved).at[2:2 + 2 * twos:2].set(receiver + moved)
    return sizes[jax.random.permutation(jax.random.fold_in(own_key, 2), amount)]


def routed_block(stream_key, own, number, rows, count, top, reach, lean):
    ranking = jax.random.permutation(stream_key, count)
    packed, common = load_shares(count, rows * top, reach, lean, True), load_shares(count, rows * top, reach, lean, False)
    places = jnp.arange(count)

    def named(sizes, turn):
        used = int((sizes > 0).sum())
        fixed = max(1, used // 4)
        shifted = fixed + (places - fixed + turn * (used - fixed)) % max(1, count - fixed)
        return jnp.zeros((count,), jnp.int32).at[ranking[jnp.where(places < fixed, places, shifted)]].set(jnp.asarray(sizes, jnp.int32))

    sizes = jnp.where(number % 4 == 0, named(packed, number // 4), named(common, number - number // 4 - 1))
    mixed = jax.random.permutation(jax.random.fold_in(own, 3), count)
    donor, sink = mixed[0:count // 2 * 2:2], mixed[1:count // 2 * 2:2]
    margin = jnp.minimum(sizes[donor] - 1, reach - sizes[sink]) // 2
    margin = jnp.where((donor == ranking[0]) | (sink == ranking[0]) | (sizes[sink] == 0), 0, jnp.maximum(margin, 0))
    shifted = jax.random.randint(jax.random.fold_in(own, 4), (count // 2,), 0, 1 << 20) % (margin + 1)
    sizes = sizes.at[donor].add(-shifted).at[sink].add(shifted)
    members = jnp.searchsorted(jnp.cumsum(sizes), jnp.arange(rows * top), side="right").astype(jnp.int32)
    table = members.reshape(top, rows).T
    table = table[jax.random.permutation(jax.random.fold_in(own, 1), rows)]
    turn = jax.random.randint(jax.random.fold_in(own, 2), (rows, 1), 0, top)
    return jnp.take_along_axis(table, (jnp.arange(top)[None, :] + turn) % top, axis=1)


def load_shares(number_of, total, reach, skew, full):
    weights = [(1 << 20) // math.isqrt(grade ** skew) + 1 for grade in range(1, number_of + 1)]
    largest = reach if full else min(reach, max(-(-total // number_of), total * weights[0] // sum(weights)))
    least = 1 if total - largest >= number_of - 1 else 0
    given, rest = [largest] + [least] * (number_of - 1), total - largest - least * (number_of - 1)
    while rest > 0:
        movable = [i for i in range(1, number_of) if given[i] < largest] or [i for i in range(1, number_of) if given[i] < reach]
        whole, left = sum([weights[i] for i in movable]), rest
        for i in movable:
            extra = min(reach - given[i], max(1, left * weights[i] // whole), rest)
            given[i] = given[i] + extra
            rest = rest - extra
    return np.array(given)


def scatter_about(own_key, shape, width, limit, cuts=(), kind=jnp.bfloat16):
    result = width * jax.random.normal(own_key, shape, jnp.float32)
    if cuts:
        result = result * levels(own_key, shape, cuts, -0.22, 0.18)
    return jnp.clip(result, -limit, limit).astype(kind)


def setup_inputs(seed: int = 0) -> dict:
    seeds = jax.random.split(jax.random.key(seed), 11)
    hidden = scatter_about(seeds[0], (N_GRP, RESPONSE_ROWS, D), 1.0, 6.0, ((0, 8), (1, 32)))
    queries = draw_queries(jax.random.fold_in(seeds[10], 71), 0)
    response_key_value = scatter_about(seeds[2], (N_GRP, RESPONSE_ROWS, 2 * KEY_VALUE_HEADS * HEAD_SIZE), 1.0, 6.0, ((0, 8), (1, 32)))
    prompt_kv = draw_prompt_kv(jax.random.fold_in(seeds[10], 71), 0)
    lengths = jax.vmap(lambda own: ragged_sizes(own, GROUP_RESPONSES, GROUP_RESPONSES * RESPONSE_LENGTH * 3 // 4, RESPONSE_LENGTH, 2))(jax.random.split(seeds[4], N_GRP)).reshape((N_GRP, GROUP_RESPONSES)).astype(jnp.int32)
    out_weight = scatter_about(seeds[5], (QUERY_HEADS * HEAD_SIZE, D), (QUERY_HEADS * HEAD_SIZE) ** -0.5, 0.09375, ((0, 8), (1, 32)))
    norm_gain = jnp.clip(1.0 + 0.1 * jax.random.normal(seeds[6], (D,), jnp.float32), 0.5, 1.5)
    router = scatter_about(seeds[7], (D, EXPERTS), (3 * D // 2) ** -0.5, 0.078125)
    gate_up = scatter_about(seeds[8], (SLICES, D, FF), D ** -0.5, 0.09375, ((0, 256),))
    routes_keys = jax.random.split(jax.random.fold_in(seeds[9], 1), N_GRP * RESPONSE_ROWS // TOK_DEV)
    routes_turns = jax.random.permutation(jax.random.fold_in(seeds[9], 3), N_GRP * RESPONSE_ROWS // TOK_DEV)
    routes = jax.vmap(lambda own, number: routed_block(jax.random.fold_in(seeds[9], 2), own, number, TOK_DEV, EXPERTS, ROUTES, CAP, 2))(routes_keys, routes_turns).reshape((N_GRP, RESPONSE_ROWS, ROUTES))
    return dict(hidden=hidden, queries=queries, response_key_value=response_key_value, prompt_kv=prompt_kv, lengths=lengths, out_weight=out_weight, norm_gain=norm_gain, router=router, gate_up=gate_up, routes=routes)


def attend_group(operands):
    group_query, group_key_value, prompt_of_group, group_len = operands
    heads_per_key_value = QUERY_HEADS // KEY_VALUE_HEADS
    scale_qk = HEAD_SIZE ** (-0.5)
    query_everything = group_query.reshape(GROUP_RESPONSES, RESPONSE_LENGTH, KEY_VALUE_HEADS, heads_per_key_value, HEAD_SIZE).astype(jnp.float32)
    own_key_value = group_key_value.reshape(GROUP_RESPONSES, RESPONSE_LENGTH, 2, KEY_VALUE_HEADS, HEAD_SIZE).astype(jnp.float32)
    prompt_everything = prompt_of_group.reshape(PROMPT_LENGTH, 2, KEY_VALUE_HEADS, HEAD_SIZE).astype(jnp.float32)
    prompt_scores = jnp.einsum('rtkgd,skd->rkgts', query_everything, prompt_everything[:, 0]) * scale_qk
    own_scores = jnp.einsum('rtkgd,rskd->rkgts', query_everything, own_key_value[:, :, 0]) * scale_qk
    position = jnp.arange(RESPONSE_LENGTH, dtype=jnp.int32)
    allowed = (position[None, None, :] <= position[None, :, None]) & (position[None, None, :] < group_len[:, None, None])
    own_scores = jnp.where(allowed[:, None, None], own_scores, -1e+30)
    weights_all = jax.nn.softmax(jnp.concatenate([prompt_scores, own_scores], axis=-1), axis=-1)
    context = jnp.einsum('rkgts,skd->rtkgd', weights_all[..., :PROMPT_LENGTH], prompt_everything[:, 1])
    context = context + jnp.einsum('rkgts,rskd->rtkgd', weights_all[..., PROMPT_LENGTH:], own_key_value[:, :, 1])
    return context.reshape(RESPONSE_ROWS, QUERY_HEADS * HEAD_SIZE).astype(jnp.bfloat16)

def reference(hidden, queries, response_key_value, prompt_kv, lengths, out_weight, norm_gain, router, gate_up, routes):
    context = lax.map(attend_group, (queries, response_key_value, prompt_kv, lengths))
    head_width = QUERY_HEADS * HEAD_SIZE // N_GRP

    def project(context_rows):
        summed = jnp.zeros((RESPONSE_ROWS, D), jnp.float32)
        for head_set in range(N_GRP):
            lo_col = head_set * head_width
            partial_rows = jnp.dot(context_rows[:, lo_col:lo_col + head_width], out_weight[lo_col:lo_col + head_width], preferred_element_type=jnp.float32)
            summed = summed + lax.optimization_barrier(partial_rows.astype(jnp.bfloat16)).astype(jnp.float32)
        return summed
    attention = lax.map(project, context)
    resid_out = (hidden.astype(jnp.float32) + attention).astype(jnp.bfloat16)
    resid_f = resid_out.astype(jnp.float32)
    normed = (resid_f * lax.rsqrt(lax.optimization_barrier(jnp.mean(resid_f * resid_f, axis=-1, keepdims=True)) + 1e-06) * norm_gain).astype(jnp.bfloat16)
    normed_src = normed.reshape(SOURCES, TOK_DEV, D)
    route_src = routes.reshape(SOURCES, TOK_DEV, ROUTES)

    def block_weights(operands):
        block_rows, block_routes = operands
        logits = jnp.dot(block_rows, router, preferred_element_type=jnp.float32)
        chosen = jnp.take_along_axis(logits, block_routes, axis=1)
        return jax.nn.softmax(chosen, axis=-1).astype(jnp.bfloat16).reshape(TOK_DEV * ROUTES)
    weight_src = lax.map(block_weights, (normed_src, route_src))
    flat_ids = route_src.reshape(SOURCES, TOK_DEV * ROUTES)
    one_hot = (flat_ids[..., None] == jnp.arange(EXPERTS, dtype=jnp.int32)).astype(jnp.int32)
    rank_rows = jnp.cumsum(one_hot, axis=1) - one_hot
    slot_ids = lax.optimization_barrier(jnp.sum(rank_rows * one_hot, axis=-1))
    source_ids = jnp.broadcast_to(jnp.arange(SOURCES, dtype=jnp.int32)[:, None], flat_ids.shape)
    pair_ids = jnp.broadcast_to(jnp.arange(TOK_DEV * ROUTES, dtype=jnp.int32)[None, :], flat_ids.shape)
    pair_table = jnp.full((SOURCES, EXPERTS, CAP), -1, jnp.int32).at[source_ids, flat_ids, slot_ids].set(pair_ids)

    def expert_rows(expert_id):
        pairs = lax.dynamic_index_in_dim(pair_table, expert_id, 1, keepdims=False)
        filled = pairs >= 0
        safe_ids = jnp.where(filled, pairs, 0)
        token_rows = jnp.take_along_axis(normed_src, (safe_ids // ROUTES)[..., None], axis=1)
        token_rows = jnp.where(filled[..., None], token_rows, jnp.zeros((), jnp.bfloat16)).reshape(SOURCES * CAP, D)
        scale_rows = jnp.where(filled, jnp.take_along_axis(weight_src, safe_ids, axis=1).astype(jnp.float32), 0.0).reshape(SOURCES * CAP, 1)
        halves = lax.dynamic_slice_in_dim(gate_up, 2 * expert_id, 2, 0)
        results = []
        for half in range(2):
            mixed = jnp.dot(token_rows, halves[half], preferred_element_type=jnp.float32)
            active = scale_rows * jax.nn.silu(mixed[:, :FFH]) * mixed[:, FFH:]
            results.append(active.astype(jnp.bfloat16).reshape(SOURCES, CAP, FFH))
        return jnp.stack(results)
    expert_act = lax.map(expert_rows, jnp.arange(EXPERTS, dtype=jnp.int32)).reshape(SLICES, SOURCES, CAP, FFH)
    return (resid_out, expert_act)
```

```python
import jax
import jax.numpy as jnp
from jax import lax
from jax.experimental import pallas as pl
from jax.experimental.pallas import tpu as pltpu
from jax.sharding import PartitionSpec as P

QUERY_HEADS = 32
KEY_VALUE_HEADS = 2
HEAD_SIZE = 128
ROUTES = 4


neg_fill = -1e30
eps_norm = 1e-06


MESH = pl.DeviceIdType.MESH
NX, NY, NZ = 4, 4, 8
CHUNKS = 8
CAP = 6
PEERS = NX * NY
PEER_ROWS = NZ * CAP
SLOT_ROWS = PEERS * PEER_ROWS


def position():
    g, i = lax.axis_index("grp"), lax.axis_index("exp")
    x, y_hi = lax.div(g, 2), lax.rem(g, 2)
    z, y_lo, core = lax.div(i, 4), lax.rem(lax.div(i, 2), 2), lax.rem(i, 2)
    return x, y_hi * 2 + y_lo, z, core


def device(x, y, z, core):
    return (x * 2 + lax.div(y, 2), (z * 2 + lax.rem(y, 2)) * 2 + core)


def remote(src, dst, send, recv, to):
    return pltpu.make_async_remote_copy(
        src_ref=src, dst_ref=dst, send_sem=send, recv_sem=recv, device_id=to, device_id_type=MESH
    )


def wait_bytes(ref, sem):
    pltpu.make_async_copy(ref, ref, sem).wait()


def dispatch_kernel(
    x_ref,
    rw_ref,
    gu_ref,
    out_ref,
    xall,
    rwall,
    wbuf,
    sel,
    sendb,
    recvb,
    wsend,
    wrecv,
    acc,
    outsend,
    z_right,
    z_left,
    z_send,
    rw_right,
    rw_left,
    rw_send,
    p_send,
    p_recv,
    w_sems,
    gu_sems,
    out_sems,
):
    x, y, z, core = position()
    up, down = lax.rem(z + 1, NZ), lax.rem(z + NZ - 1, NZ)
    up_dev, down_dev = device(x, y, up, core), device(x, y, down, core)
    sibling = device(x, y, z, 1 - core)
    mine = x * NY + y
    width = x_ref.shape[1] // CHUNKS

    def peer(d):
        px = lax.rem(x + lax.div(d, NY), NX)
        py = lax.rem(y + lax.rem(d, NY), NY)
        return px * NY + py, device(px, py, z, core)

    barrier = pltpu.get_barrier_semaphore()
    for to in (up_dev, down_dev, sibling):
        pl.semaphore_signal(barrier, inc=1, device_id=to, device_id_type=MESH)

    def greet(d, carry):
        pl.semaphore_signal(barrier, inc=1, device_id=peer(d)[1], device_id_type=MESH)
        return carry

    lax.fori_loop(1, PEERS, greet, 0)
    pl.semaphore_wait(barrier, 3 + PEERS - 1)

    def rw_hop(step, right):
        if right:
            block, to, sem = lax.rem(z + NZ - step, NZ), up_dev, rw_right
        else:
            block, to, sem = lax.rem(z + step, NZ), down_dev, rw_left
        return remote(rwall.at[block], rwall.at[block], rw_send.at[0], sem.at[step], to)

    def hop(k, step, right):
        if right:
            block, to, sem = lax.rem(z + NZ - step, NZ), up_dev, z_right
        else:
            block, to, sem = lax.rem(z + step, NZ), down_dev, z_left
        return remote(xall.at[k, block], xall.at[k, block], z_send.at[k], sem.at[k, step], to)

    rwall[z] = rw_ref[...]
    rw_hop(0, True).start()
    rw_hop(0, False).start()
    own_copy = pltpu.make_async_copy(gu_ref, wbuf.at[core], gu_sems.at[0])
    own_copy.start()
    other_copy = remote(gu_ref, wbuf.at[core], gu_sems.at[1], gu_sems.at[2], sibling)
    for k in range(CHUNKS):
        xall[k, z] = x_ref[:, k * width : (k + 1) * width]
        if k < 2:
            hop(k, 0, True).start()
            hop(k, 0, False).start()
        if k == 1:
            other_copy.start()

    def zero(r, carry):
        acc[lax.div(r, 3), pl.ds(pl.multiple_of(lax.rem(r, 3) * 256, 256), 256), :] = jnp.zeros(
            (256, acc.shape[2]), jnp.float32
        )
        return carry

    lax.fori_loop(0, 6, zero, 0)

    def tick(t, carry):
        @pl.when((t >= 1) & (t <= 4))
        def _():
            rw_hop(t - 1, True).wait_recv()

            @pl.when(t < 4)
            def _():
                rw_hop(t - 1, False).wait_recv()
                rw_hop(t, True).start()

            @pl.when(t < 3)
            def _():
                rw_hop(t, False).start()

        for step in (4, 3, 2, 1):
            k = t - step

            @pl.when((k >= 0) & (k < CHUNKS))
            def _():
                even = lax.rem(k, 2) == 0
                if step == 4:

                    @pl.when(even)
                    def _():
                        hop(k, 3, True).wait_recv()

                    @pl.when(jnp.logical_not(even))
                    def _():
                        hop(k, 3, False).wait_recv()
                else:
                    hop(k, step - 1, True).wait_recv()
                    if step < 3:
                        hop(k, step, True).start()
                    else:

                        @pl.when(even)
                        def _():
                            hop(k, step, True).start()

                    hop(k, step - 1, False).wait_recv()
                    if step < 3:
                        hop(k, step, False).start()
                    else:

                        @pl.when(jnp.logical_not(even))
                        def _():
                            hop(k, step, False).start()

        @pl.when(t + 2 < CHUNKS)
        def _():
            hop(t + 2, 0, True).start()
            hop(t + 2, 0, False).start()

        @pl.when(t == 4)
        def _():
            row = lax.broadcasted_iota(jnp.int32, (SLOT_ROWS, 1), 0).astype(jnp.float32)
            place = jnp.floor((row + 0.5) * (1.0 / PEER_ROWS))
            within = row - place * PEER_ROWS
            source = jnp.floor((within + 0.5) * (1.0 / CAP))
            slot = within - source * CAP
            px = jnp.floor((place + 0.5) * 0.25)
            py = place - px * 4
            py_hi = jnp.floor((py + 0.5) * 0.5)
            expert = px * 32 + py_hi * 16 + (py - py_hi * 2) + (z * 2).astype(jnp.float32)
            lane = lax.broadcasted_iota(jnp.int32, (SLOT_ROWS, 128), 1).astype(jnp.float32)
            chosen = (lane == expert).astype(jnp.bfloat16)
            total = jnp.zeros((SLOT_ROWS, 128), jnp.float32)
            dims = (((1,), (1,)), ((), ()))
            for b in range(NZ):
                ranks = lax.dot_general(chosen, rwall[b, :, :128], dims, preferred_element_type=jnp.float32)
                weights = lax.dot_general(chosen, rwall[b, :, 128:], dims, preferred_element_type=jnp.float32)
                hit = (ranks == slot + 1.0) & (source == float(b))
                sel[:, b * 128 : (b + 1) * 128] = hit.astype(jnp.bfloat16)
                total = total + jnp.where(hit, weights, 0.0)
            wsend[...] = jnp.broadcast_to(jnp.sum(total, axis=1, keepdims=True), (SLOT_ROWS, 128)).astype(
                jnp.bfloat16
            )
            own = pl.ds(pl.multiple_of(mine * PEER_ROWS, 16), PEER_ROWS)
            wrecv[own, :] = wsend[own, :]

            def send(d, c):
                p, to = peer(d)
                there = pl.ds(pl.multiple_of(p * PEER_ROWS, 16), PEER_ROWS)
                remote(wsend.at[there], wrecv.at[own], w_sems.at[0], w_sems.at[1], to).start()
                return c

            lax.fori_loop(1, PEERS, send, 0)

        k_sel = t - 4

        @pl.when((k_sel >= 0) & (k_sel < CHUNKS))
        def _():
            own = pl.ds(pl.multiple_of(mine * PEER_ROWS, 16), PEER_ROWS)

            def pick(r, c):
                rows = pl.ds(pl.multiple_of(r * 256, 256), 256)
                picked = jnp.dot(
                    sel[rows, :],
                    xall[k_sel].reshape(NZ * 128, width),
                    preferred_element_type=jnp.float32,
                )
                sendb[k_sel, rows, :] = picked.astype(jnp.bfloat16)
                return c

            lax.fori_loop(0, SLOT_ROWS // 256, pick, 0)

            def send(d, c):
                p, to = peer(d)
                there = pl.ds(pl.multiple_of(p * PEER_ROWS, 16), PEER_ROWS)
                remote(
                    sendb.at[k_sel, there], recvb.at[k_sel, own], p_send.at[k_sel], p_recv.at[k_sel], to
                ).start()
                return c

            lax.fori_loop(1, PEERS, send, 0)
            recvb[k_sel, own, :] = sendb[k_sel, own, :]

        k_mul = t - 5

        @pl.when(k_mul >= 0)
        def _():
            @pl.when(k_mul == 0)
            def _():
                own_copy.wait()
                other_copy.wait_recv()

            wait_bytes(recvb.at[k_mul, pl.ds(0, SLOT_ROWS - PEER_ROWS)], p_recv.at[k_mul])
            cols = pl.ds(pl.multiple_of(k_mul * width, width), width)

            def multiply(r, c):
                h, rows = lax.div(r, 3), pl.ds(pl.multiple_of(lax.rem(r, 3) * 256, 256), 256)
                acc[h, rows, :] += jnp.dot(
                    recvb[k_mul, rows, :], wbuf[h, cols, :], preferred_element_type=jnp.float32
                )
                return c

            lax.fori_loop(0, 6, multiply, 0)

        return carry

    lax.fori_loop(0, CHUNKS + 5, tick, 0)

    wait_bytes(wrecv.at[pl.ds(0, SLOT_ROWS - PEER_ROWS)], w_sems.at[1])
    half = acc.shape[2] // 2

    def finish(h, rows):
        gate, lift = acc[h, rows, :half], acc[h, rows, half:]
        weight = wrecv[rows, :1].astype(jnp.float32)
        return (weight * (gate / (1.0 + jnp.exp(-gate))) * lift).astype(jnp.bfloat16)

    def finish_other(r, c):
        rows = pl.ds(pl.multiple_of(r * 256, 256), 256)
        outsend[rows, :] = finish(1 - core, rows)
        return c

    def finish_own(r, c):
        rows = pl.ds(pl.multiple_of(r * 256, 256), 256)
        out_ref[core, rows, :] = finish(core, rows)
        return c

    lax.fori_loop(0, SLOT_ROWS // 256, finish_other, 0)
    out_copy = remote(outsend, out_ref.at[core], out_sems.at[0], out_sems.at[1], sibling)
    out_copy.start()
    lax.fori_loop(0, SLOT_ROWS // 256, finish_own, 0)

    def drain(k, c):
        wait_bytes(xall.at[k, pl.ds(0, NZ - 1)], z_send.at[k])
        wait_bytes(sendb.at[k, pl.ds(0, SLOT_ROWS - PEER_ROWS)], p_send.at[k])
        return c

    lax.fori_loop(0, CHUNKS, drain, 0)
    wait_bytes(rwall.at[pl.ds(0, NZ - 1)], rw_send.at[0])
    wait_bytes(wsend.at[pl.ds(0, SLOT_ROWS - PEER_ROWS)], w_sems.at[0])
    other_copy.wait_send()
    out_copy.wait()


def dispatch(normed, rank_weight, gate_up):
    tokens, model = normed.shape
    width = model // CHUNKS
    inner = gate_up.shape[1]
    vmem = pl.BlockSpec(memory_space=pltpu.VMEM)
    dma = pltpu.SemaphoreType.DMA
    return pl.pallas_call(
        dispatch_kernel,
        out_shape=jax.ShapeDtypeStruct((2, SLOT_ROWS, inner // 2), jnp.bfloat16),
        in_specs=[vmem, vmem, pl.BlockSpec(memory_space=pl.ANY)],
        out_specs=vmem,
        scratch_shapes=[
            pltpu.VMEM((CHUNKS, NZ, tokens, width), jnp.bfloat16),
            pltpu.VMEM((NZ, tokens, 256), jnp.bfloat16),
            pltpu.VMEM((2, model, inner), jnp.bfloat16),
            pltpu.VMEM((SLOT_ROWS, NZ * tokens), jnp.bfloat16),
            pltpu.VMEM((CHUNKS, SLOT_ROWS, width), jnp.bfloat16),
            pltpu.VMEM((CHUNKS, SLOT_ROWS, width), jnp.bfloat16),
            pltpu.VMEM((SLOT_ROWS, 128), jnp.bfloat16),
            pltpu.VMEM((SLOT_ROWS, 128), jnp.bfloat16),
            pltpu.VMEM((2, SLOT_ROWS, inner), jnp.float32),
            pltpu.VMEM((SLOT_ROWS, inner // 2), jnp.bfloat16),
            dma((CHUNKS, 4)),
            dma((CHUNKS, 4)),
            dma((CHUNKS,)),
            dma((4,)),
            dma((4,)),
            dma((1,)),
            dma((CHUNKS,)),
            dma((CHUNKS,)),
            dma((2,)),
            dma((3,)),
            dma((2,)),
        ],
        compiler_params=pltpu.CompilerParams(
            collective_id=1, has_side_effects=True, vmem_limit_bytes=60 * 1024 * 1024
        ),
        cost_estimate=pl.CostEstimate(
            flops=2 * SLOT_ROWS * model * (2 * inner + NZ * tokens),
            bytes_accessed=model * inner * 2,
            transcendentals=0,
        ),
        name="dispatch",
    )(normed, rank_weight, gate_up)


def passed_along(array, axis, by):
    peers = lax.axis_size(axis)
    pairs = [(i, i + by) for i in range(peers) if 0 <= i + by < peers]
    return lax.ppermute(array, axis, pairs)


def local(
    hidden,
    queries,
    response_key_value,
    prompt_kv,
    lengths,
    out_weight,
    norm_gain,
    router,
    gate_up,
    routes,
):
    token_total = queries.shape[1]
    heads_per_key_value = QUERY_HEADS // KEY_VALUE_HEADS
    key_value_width = KEY_VALUE_HEADS * HEAD_SIZE
    scale_qk = HEAD_SIZE ** (-0.5)
    exp_index = lax.axis_index("exp")
    parity = exp_index % 2
    response = exp_index // 2
    length_now = lax.dynamic_index_in_dim(lengths[0], response, 0, keepdims=False)
    query_head_rows = queries[0].reshape(
        token_total, KEY_VALUE_HEADS, heads_per_key_value, HEAD_SIZE
    )
    prior_kv = passed_along(response_key_value, "exp", 1)
    joined_key_value = jnp.concatenate([prior_kv[0], response_key_value[0]], axis=0)
    key_portion = joined_key_value[:, :key_value_width].reshape(
        2 * token_total, KEY_VALUE_HEADS, HEAD_SIZE
    )
    value_portion = (
        joined_key_value[:, key_value_width:]
        .reshape(2 * token_total, KEY_VALUE_HEADS, HEAD_SIZE)
        .astype(jnp.float32)
    )
    step_ids = jnp.arange(token_total, dtype=jnp.int32)
    query_pos = parity * token_total + step_ids
    key_pos = jnp.concatenate([step_ids, parity * token_total + step_ids])
    from_prior = jnp.arange(2 * token_total, dtype=jnp.int32) < token_total
    allowed = (
        (key_pos[None, :] <= query_pos[:, None])
        & (key_pos < length_now)[None, :]
        & (~from_prior | (parity == 1))[None, :]
    )
    own_scores = (
        jnp.einsum(
            "tkgd,skd->kgts", query_head_rows, key_portion, preferred_element_type=jnp.float32
        )
        * scale_qk
    )
    own_scores = jnp.where(allowed[None, None], own_scores, neg_fill)
    whole_prompt = lax.all_gather(prompt_kv, "exp", axis=1, tiled=True)[0]
    prompt_count = whole_prompt.shape[0]
    prompt_keys = whole_prompt[:, :key_value_width].reshape(
        prompt_count, KEY_VALUE_HEADS, HEAD_SIZE
    )
    prompt_values = (
        whole_prompt[:, key_value_width:]
        .reshape(prompt_count, KEY_VALUE_HEADS, HEAD_SIZE)
        .astype(jnp.float32)
    )
    prompt_scores = (
        jnp.einsum(
            "tkgd,skd->kgts", query_head_rows, prompt_keys, preferred_element_type=jnp.float32
        )
        * scale_qk
    )
    row_top = jnp.maximum(jnp.max(own_scores, axis=-1), jnp.max(prompt_scores, axis=-1))
    own_probs = jnp.exp(own_scores - row_top[..., None])
    prompt_probs = jnp.exp(prompt_scores - row_top[..., None])
    denom_sum = jnp.sum(own_probs, axis=-1) + jnp.sum(prompt_probs, axis=-1)
    weighted = jnp.einsum("kgts,skd->kgtd", own_probs, value_portion) + jnp.einsum(
        "kgts,skd->kgtd", prompt_probs, prompt_values
    )
    context = (
        (weighted / denom_sum[..., None])
        .transpose(2, 0, 1, 3)
        .reshape(token_total, QUERY_HEADS * HEAD_SIZE)
        .astype(jnp.bfloat16)
    )
    n_grp = lax.axis_size("grp")
    traded = lax.all_to_all(
        context.reshape(token_total, n_grp, QUERY_HEADS * HEAD_SIZE // n_grp),
        "grp",
        split_axis=1,
        concat_axis=1,
        tiled=True,
    )
    left_rows = traded.reshape(token_total * n_grp, QUERY_HEADS * HEAD_SIZE // n_grp)
    projected = jnp.dot(
        left_rows,
        lax.all_gather(out_weight, "exp", axis=1, tiled=True),
        preferred_element_type=jnp.float32,
    ).astype(jnp.bfloat16)
    attention = (
        lax.psum_scatter(
            projected.reshape(token_total, n_grp, -1).astype(jnp.float32).astype(jnp.bfloat16),
            "grp",
            scatter_dimension=1,
            tiled=True,
        )
        .astype(jnp.float32)
        .reshape(token_total, -1)
    )
    resid_out = (hidden[0].astype(jnp.float32) + attention).astype(jnp.bfloat16)
    resid_f = resid_out.astype(jnp.float32)
    normed = (
        resid_f
        * lax.rsqrt(jnp.mean(resid_f * resid_f, axis=-1, keepdims=True) + eps_norm)
        * norm_gain
    ).astype(jnp.bfloat16)
    experts = router.shape[1]
    logits = jnp.dot(normed, router, preferred_element_type=jnp.float32)
    named = jnp.any(
        routes[0][:, :, None] == jnp.arange(experts, dtype=jnp.int32)[None, None, :], axis=1
    )
    masked = jnp.where(named, logits, neg_fill)
    raised = jnp.where(named, jnp.exp(masked - jnp.max(masked, axis=1, keepdims=True)), 0.0)
    route_weight = (raised / jnp.sum(raised, axis=1, keepdims=True)).astype(jnp.bfloat16)
    earlier = step_ids[:, None] >= step_ids[None, :]
    ranks = jnp.dot(
        earlier.astype(jnp.bfloat16), named.astype(jnp.bfloat16), preferred_element_type=jnp.float32
    )
    ranks = jnp.where(named, ranks, 0.0).astype(jnp.bfloat16)
    slots = dispatch(normed, jnp.concatenate([ranks, route_weight], axis=1), gate_up[0])
    expert_act = (
        slots.reshape(2, NX, 2, 2, NZ, CAP, -1)
        .transpose(1, 2, 4, 3, 0, 5, 6)
        .reshape(1, 2 * NX * NZ * NY, CAP, -1)
    )
    return (resid_out[None], expert_act)


def solution(mesh):
    placed = (
        P("grp", "exp", None),
        P("grp", "exp", None),
        P("grp", "exp", None),
        P("grp", "exp", None),
        P("grp", None),
        P("grp", "exp"),
        P(),
        P(),
        P(("grp", "exp"), None, None),
        P("grp", "exp", None),
    )
    return jax.shard_map(
        local,
        mesh=mesh,
        in_specs=placed,
        out_specs=(P("grp", "exp", None), P(("grp", "exp"), None, None, None)),
        check_vma=False,
    )
```

```python
import jax
import jax.numpy as jnp
from jax import lax
from jax.experimental import pallas as pl
from jax.experimental.pallas import tpu as pltpu
from jax.sharding import PartitionSpec as P

QUERY_HEADS = 32
KEY_VALUE_HEADS = 2
HEAD_SIZE = 128


neg_fill = -1e30
eps_norm = 1e-06


MESH = pl.DeviceIdType.MESH
NX, NY, NZ = 4, 4, 8
CHUNKS = 8
CAP = 6
PEERS = NX * NY
PEER_ROWS = NZ * CAP
SLOT_ROWS = PEERS * PEER_ROWS


def position():
    g, i = lax.axis_index("grp"), lax.axis_index("exp")
    x, y_hi = lax.div(g, 2), lax.rem(g, 2)
    z, y_lo, core = lax.div(i, 4), lax.rem(lax.div(i, 2), 2), lax.rem(i, 2)
    return x, y_hi * 2 + y_lo, z, core


def device(x, y, z, core):
    return (x * 2 + lax.div(y, 2), (z * 2 + lax.rem(y, 2)) * 2 + core)


def remote(src, dst, send, recv, to):
    return pltpu.make_async_remote_copy(
        src_ref=src, dst_ref=dst, send_sem=send, recv_sem=recv, device_id=to, device_id_type=MESH
    )


def wait_bytes(ref, sem):
    pltpu.make_async_copy(ref, ref, sem).wait()


def dispatch_kernel(
    x_ref,
    rw_ref,
    gu_ref,
    out_ref,
    xall,
    rwall,
    wbuf,
    sel,
    sendb,
    recvb,
    wsend,
    wrecv,
    acc,
    outsend,
    z_right,
    z_left,
    z_send,
    rw_right,
    rw_left,
    rw_send,
    p_send,
    p_recv,
    w_sems,
    gu_sems,
    out_sems,
):
    x, y, z, core = position()
    up, down = lax.rem(z + 1, NZ), lax.rem(z + NZ - 1, NZ)
    up_dev, down_dev = device(x, y, up, core), device(x, y, down, core)
    sibling = device(x, y, z, 1 - core)
    mine = x * NY + y
    width = x_ref.shape[1] // CHUNKS

    def peer(d):
        px = lax.rem(x + lax.div(d, NY), NX)
        py = lax.rem(y + lax.rem(d, NY), NY)
        return px * NY + py, device(px, py, z, core)

    barrier = pltpu.get_barrier_semaphore()
    for to in (up_dev, down_dev, sibling):
        pl.semaphore_signal(barrier, inc=1, device_id=to, device_id_type=MESH)

    def greet(d, carry):
        pl.semaphore_signal(barrier, inc=1, device_id=peer(d)[1], device_id_type=MESH)
        return carry

    lax.fori_loop(1, PEERS, greet, 0)
    pl.semaphore_wait(barrier, 3 + PEERS - 1)

    def rw_hop(step, right):
        if right:
            block, to, sem = lax.rem(z + NZ - step, NZ), up_dev, rw_right
        else:
            block, to, sem = lax.rem(z + step, NZ), down_dev, rw_left
        return remote(rwall.at[block], rwall.at[block], rw_send.at[0], sem.at[step], to)

    def hop(k, step, right):
        if right:
            block, to, sem = lax.rem(z + NZ - step, NZ), up_dev, z_right
        else:
            block, to, sem = lax.rem(z + step, NZ), down_dev, z_left
        return remote(xall.at[k, block], xall.at[k, block], z_send.at[k], sem.at[k, step], to)

    rwall[z] = rw_ref[...]
    rw_hop(0, True).start()
    rw_hop(0, False).start()
    own_copy = pltpu.make_async_copy(gu_ref, wbuf.at[core], gu_sems.at[0])
    own_copy.start()
    other_copy = remote(gu_ref, wbuf.at[core], gu_sems.at[1], gu_sems.at[2], sibling)
    for k in range(CHUNKS):
        xall[k, z] = x_ref[:, k * width : (k + 1) * width]
        if k < 2:
            hop(k, 0, True).start()
            hop(k, 0, False).start()
        if k == 1:
            other_copy.start()

    def zero(r, carry):
        acc[lax.div(r, 3), pl.ds(pl.multiple_of(lax.rem(r, 3) * 256, 256), 256), :] = jnp.zeros(
            (256, acc.shape[2]), jnp.float32
        )
        return carry

    lax.fori_loop(0, 6, zero, 0)

    def tick(t, carry):
        @pl.when((t >= 1) & (t <= 4))
        def _():
            rw_hop(t - 1, True).wait_recv()

            @pl.when(t < 4)
            def _():
                rw_hop(t - 1, False).wait_recv()
                rw_hop(t, True).start()

            @pl.when(t < 3)
            def _():
                rw_hop(t, False).start()

        for step in (4, 3, 2, 1):
            k = t - step

            @pl.when((k >= 0) & (k < CHUNKS))
            def _():
                even = lax.rem(k, 2) == 0
                if step == 4:

                    @pl.when(even)
                    def _():
                        hop(k, 3, True).wait_recv()

                    @pl.when(jnp.logical_not(even))
                    def _():
                        hop(k, 3, False).wait_recv()
                else:
                    hop(k, step - 1, True).wait_recv()
                    if step < 3:
                        hop(k, step, True).start()
                    else:

                        @pl.when(even)
                        def _():
                            hop(k, step, True).start()

                    hop(k, step - 1, False).wait_recv()
                    if step < 3:
                        hop(k, step, False).start()
                    else:

                        @pl.when(jnp.logical_not(even))
                        def _():
                            hop(k, step, False).start()

        @pl.when(t + 2 < CHUNKS)
        def _():
            hop(t + 2, 0, True).start()
            hop(t + 2, 0, False).start()

        @pl.when(t == 4)
        def _():
            row = lax.broadcasted_iota(jnp.int32, (SLOT_ROWS, 1), 0).astype(jnp.float32)
            place = jnp.floor((row + 0.5) * (1.0 / PEER_ROWS))
            within = row - place * PEER_ROWS
            source = jnp.floor((within + 0.5) * (1.0 / CAP))
            slot = within - source * CAP
            px = jnp.floor((place + 0.5) * 0.25)
            py = place - px * 4
            py_hi = jnp.floor((py + 0.5) * 0.5)
            expert = px * 32 + py_hi * 16 + (py - py_hi * 2) + (z * 2).astype(jnp.float32)
            lane = lax.broadcasted_iota(jnp.int32, (SLOT_ROWS, 128), 1).astype(jnp.float32)
            chosen = (lane == expert).astype(jnp.bfloat16)
            total = jnp.zeros((SLOT_ROWS, 128), jnp.float32)
            dims = (((1,), (1,)), ((), ()))
            for b in range(NZ):
                ranks = lax.dot_general(chosen, rwall[b, :, :128], dims, preferred_element_type=jnp.float32)
                weights = lax.dot_general(chosen, rwall[b, :, 128:], dims, preferred_element_type=jnp.float32)
                hit = (ranks == slot + 1.0) & (source == float(b))
                sel[:, b * 128 : (b + 1) * 128] = hit.astype(jnp.bfloat16)
                total = total + jnp.where(hit, weights, 0.0)
            wsend[...] = jnp.broadcast_to(jnp.sum(total, axis=1, keepdims=True), (SLOT_ROWS, 128)).astype(
                jnp.bfloat16
            )
            own = pl.ds(pl.multiple_of(mine * PEER_ROWS, 16), PEER_ROWS)
            wrecv[own, :] = wsend[own, :]

            def send(d, c):
                p, to = peer(d)
                there = pl.ds(pl.multiple_of(p * PEER_ROWS, 16), PEER_ROWS)
                remote(wsend.at[there], wrecv.at[own], w_sems.at[0], w_sems.at[1], to).start()
                return c

            lax.fori_loop(1, PEERS, send, 0)

        k_sel = t - 4

        @pl.when((k_sel >= 0) & (k_sel < CHUNKS))
        def _():
            own = pl.ds(pl.multiple_of(mine * PEER_ROWS, 16), PEER_ROWS)

            def pick(r, c):
                rows = pl.ds(pl.multiple_of(r * 256, 256), 256)
                picked = jnp.dot(
                    sel[rows, :],
                    xall[k_sel].reshape(NZ * 128, width),
                    preferred_element_type=jnp.float32,
                )
                sendb[k_sel, rows, :] = picked.astype(jnp.bfloat16)
                return c

            lax.fori_loop(0, SLOT_ROWS // 256, pick, 0)

            def send(d, c):
                p, to = peer(d)
                there = pl.ds(pl.multiple_of(p * PEER_ROWS, 16), PEER_ROWS)
                remote(
                    sendb.at[k_sel, there], recvb.at[k_sel, own], p_send.at[k_sel], p_recv.at[k_sel], to
                ).start()
                return c

            lax.fori_loop(1, PEERS, send, 0)
            recvb[k_sel, own, :] = sendb[k_sel, own, :]

        k_mul = t - 5

        @pl.when(k_mul >= 0)
        def _():
            @pl.when(k_mul == 0)
            def _():
                own_copy.wait()
                other_copy.wait_recv()

            wait_bytes(recvb.at[k_mul, pl.ds(0, SLOT_ROWS - PEER_ROWS)], p_recv.at[k_mul])
            cols = pl.ds(pl.multiple_of(k_mul * width, width), width)

            def multiply(r, c):
                h, rows = lax.div(r, 3), pl.ds(pl.multiple_of(lax.rem(r, 3) * 256, 256), 256)
                acc[h, rows, :] += jnp.dot(
                    recvb[k_mul, rows, :], wbuf[h, cols, :], preferred_element_type=jnp.float32
                )
                return c

            lax.fori_loop(0, 6, multiply, 0)

        return carry

    lax.fori_loop(0, CHUNKS + 5, tick, 0)

    wait_bytes(wrecv.at[pl.ds(0, SLOT_ROWS - PEER_ROWS)], w_sems.at[1])
    half = acc.shape[2] // 2

    def finish(h, rows):
        gate, lift = acc[h, rows, :half], acc[h, rows, half:]
        weight = wrecv[rows, :1].astype(jnp.float32)
        return (weight * (gate / (1.0 + jnp.exp(-gate))) * lift).astype(jnp.bfloat16)

    def finish_other(r, c):
        rows = pl.ds(pl.multiple_of(r * 256, 256), 256)
        outsend[rows, :] = finish(1 - core, rows)
        return c

    def finish_own(r, c):
        rows = pl.ds(pl.multiple_of(r * 256, 256), 256)
        out_ref[core, rows, :] = finish(core, rows)
        return c

    lax.fori_loop(0, SLOT_ROWS // 256, finish_other, 0)
    out_copy = remote(outsend, out_ref.at[core], out_sems.at[0], out_sems.at[1], sibling)
    out_copy.start()
    lax.fori_loop(0, SLOT_ROWS // 256, finish_own, 0)

    def drain(k, c):
        wait_bytes(xall.at[k, pl.ds(0, NZ - 1)], z_send.at[k])
        wait_bytes(sendb.at[k, pl.ds(0, SLOT_ROWS - PEER_ROWS)], p_send.at[k])
        return c

    lax.fori_loop(0, CHUNKS, drain, 0)
    wait_bytes(rwall.at[pl.ds(0, NZ - 1)], rw_send.at[0])
    wait_bytes(wsend.at[pl.ds(0, SLOT_ROWS - PEER_ROWS)], w_sems.at[0])
    other_copy.wait_send()
    out_copy.wait()


def dispatch(normed, rank_weight, gate_up):
    tokens, model = normed.shape
    width = model // CHUNKS
    inner = gate_up.shape[1]
    vmem = pl.BlockSpec(memory_space=pltpu.VMEM)
    dma = pltpu.SemaphoreType.DMA
    return pl.pallas_call(
        dispatch_kernel,
        out_shape=jax.ShapeDtypeStruct((2, SLOT_ROWS, inner // 2), jnp.bfloat16),
        in_specs=[vmem, vmem, pl.BlockSpec(memory_space=pl.ANY)],
        out_specs=vmem,
        scratch_shapes=[
            pltpu.VMEM((CHUNKS, NZ, tokens, width), jnp.bfloat16),
            pltpu.VMEM((NZ, tokens, 256), jnp.bfloat16),
            pltpu.VMEM((2, model, inner), jnp.bfloat16),
            pltpu.VMEM((SLOT_ROWS, NZ * tokens), jnp.bfloat16),
            pltpu.VMEM((CHUNKS, SLOT_ROWS, width), jnp.bfloat16),
            pltpu.VMEM((CHUNKS, SLOT_ROWS, width), jnp.bfloat16),
            pltpu.VMEM((SLOT_ROWS, 128), jnp.bfloat16),
            pltpu.VMEM((SLOT_ROWS, 128), jnp.bfloat16),
            pltpu.VMEM((2, SLOT_ROWS, inner), jnp.float32),
            pltpu.VMEM((SLOT_ROWS, inner // 2), jnp.bfloat16),
            dma((CHUNKS, 4)),
            dma((CHUNKS, 4)),
            dma((CHUNKS,)),
            dma((4,)),
            dma((4,)),
            dma((1,)),
            dma((CHUNKS,)),
            dma((CHUNKS,)),
            dma((2,)),
            dma((3,)),
            dma((2,)),
        ],
        compiler_params=pltpu.CompilerParams(
            collective_id=1, has_side_effects=True, vmem_limit_bytes=60 * 1024 * 1024
        ),
        cost_estimate=pl.CostEstimate(
            flops=2 * SLOT_ROWS * model * (2 * inner + NZ * tokens),
            bytes_accessed=model * inner * 2,
            transcendentals=0,
        ),
        name="dispatch",
    )(normed, rank_weight, gate_up)


def attend_kernel(
    q_ref,
    kv_ref,
    prompt_ref,
    bias_ref,
    w_ref,
    hidden_ref,
    gain_ref,
    router_ref,
    ranks_ref,
    resid_ref,
    normed_ref,
    rw_ref,
    wc,
    pbuf,
    kvbuf,
    kcat,
    vcat,
    ctx,
    own_out,
    send_out,
    recv_out,
    prompt_right,
    prompt_left,
    prompt_sems,
    kv_sems,
    first_recv,
    first_send,
    z_recv,
    z_send,
    spread_send,
    x_direct,
    x_relay,
    y_direct,
    y_relay,
    ctx_sems,
    out_send,
    out_recv,
):
    x, y, z, core = position()
    y_hi, y_lo = lax.div(y, 2), lax.rem(y, 2)
    xs = [lax.rem(x + d, NX) for d in range(NX)]
    ys = [lax.rem(y + d, NY) for d in range(NY)]
    z_up, z_down = lax.rem(z + 1, NZ), lax.rem(z + NZ - 1, NZ)
    x_dev = [device(xs[d], y, z, core) for d in range(NX)]
    y_dev = [device(x, ys[d], z, core) for d in range(NY)]
    up_dev, down_dev = device(x, y, z_up, core), device(x, y, z_down, core)
    sibling = device(x, y, z, 1 - core)
    pair_dev = device(x, y_hi * 2 + 1 - y_lo, z, core)

    barrier = pltpu.get_barrier_semaphore()
    partners = x_dev[1:] + y_dev[1:] + [up_dev, down_dev, sibling]
    for to in partners:
        pl.semaphore_signal(barrier, inc=1, device_id=to, device_id_type=MESH)
    pl.semaphore_wait(barrier, len(partners))

    def prompt_hop(step, right):
        if right:
            block, to, sem = lax.rem(z + NZ - step, NZ), up_dev, prompt_right
        else:
            block, to, sem = lax.rem(z + step, NZ), down_dev, prompt_left
        part = pbuf.at[core, y_lo, block]
        return remote(part, part, prompt_sems.at[0], sem.at[step], to)

    def first(half, d):
        part = wc.at[z, y_lo, x, y_hi, half]
        to = (y_dev, x_dev)[half][d]
        return remote(part, part, first_send.at[0], first_recv.at[half, d - 1], to)

    def zpart(half, b):
        return wc.at[b, :, x, :, 0] if half == 0 else wc.at[b, y_lo, :, y_hi, 1]

    def zhop(step, right, half):
        b = lax.rem(z + (NZ - step if right else step), NZ)
        to = up_dev if right else down_dev
        return remote(
            zpart(half, b), zpart(half, b), z_send.at[0], z_recv.at[0 if right else 1, step, half], to
        )

    def xpart(b, d):
        return wc.at[b, :, xs[d], :, 0]

    def ypart(b, d):
        return wc.at[b, lax.rem(ys[d], 2), :, lax.div(ys[d], 2), 1]

    def xhalf(b, d, which):
        return wc.at[b, :, xs[d], which, 0]

    def yhalf(b, d, which):
        return wc.at[b, lax.rem(ys[d], 2), pl.ds(2 * which, 2), lax.div(ys[d], 2), 1]

    def spread(b):
        for parts, devs, sem in ((xpart, x_dev, x_direct), (ypart, y_dev, y_direct)):
            part = parts(b, 0)
            remote(part, part, spread_send.at[b], sem.at[b, 0], devs[1]).start()
            remote(part, part, spread_send.at[b], sem.at[b, 1], devs[3]).start()

    def relay(b):
        for parts, halves, devs, sem, next_sem in (
            (xpart, xhalf, x_dev, x_direct, x_relay),
            (ypart, yhalf, y_dev, y_direct, y_relay),
        ):
            wait_bytes(parts(b, 3), sem.at[b, 0])
            part = halves(b, 3, 0)
            remote(part, part, spread_send.at[b], next_sem.at[b, 0], devs[1]).start()
            wait_bytes(parts(b, 1), sem.at[b, 1])
            part = halves(b, 1, 1)
            remote(part, part, spread_send.at[b], next_sem.at[b, 1], devs[3]).start()

    def settle(b):
        for halves, next_sem in ((xhalf, x_relay), (yhalf, y_relay)):
            for which in range(2):
                wait_bytes(halves(b, 2, which), next_sem.at[b, which])

    tokens = q_ref.shape[0]

    kvbuf[core] = kv_ref[...]
    pbuf[core, y_lo, z] = prompt_ref[...]
    kv_copy = remote(kv_ref, kvbuf.at[core], kv_sems.at[0], kv_sems.at[1], sibling)
    kv_copy.start()
    prompt_hop(0, True).start()
    prompt_hop(0, False).start()
    for half in range(2):
        wc[z, y_lo, x, y_hi, half] = w_ref[half * 256 : (half + 1) * 256, :]
    for d in (1, 3, 2):
        first(0, d).start()
        first(1, d).start()
    for step in range(1, 4):
        prompt_hop(step - 1, True).wait_recv()
        prompt_hop(step, True).start()
        prompt_hop(step - 1, False).wait_recv()
        if step < 3:
            prompt_hop(step, False).start()
    for d in (1, 3, 2):
        wait_bytes(wc.at[z, lax.rem(ys[4 - d], 2), x, lax.div(ys[4 - d], 2), 0], first_recv.at[0, d - 1])
        wait_bytes(wc.at[z, y_lo, xs[4 - d], y_hi, 1], first_recv.at[1, d - 1])
    prompt_hop(3, True).wait_recv()
    part = pbuf.at[core, y_lo]
    prompt_pair = remote(part, part, prompt_sems.at[1], prompt_sems.at[2], pair_dev)
    prompt_pair.start()
    for half in range(2):
        zhop(0, True, half).start()
        zhop(0, False, half).start()
    spread(z)
    wait_bytes(pbuf.at[core, 1 - y_lo], prompt_sems.at[2])
    prompt_sib = remote(pbuf.at[core], pbuf.at[core], prompt_sems.at[3], prompt_sems.at[4], sibling)
    prompt_sib.start()
    wait_bytes(kvbuf.at[1 - core], kv_sems.at[1])

    def advance(s):
        for right in (True, False):
            for half in range(2):
                if s < 4 or half == (0 if right else 1):
                    b = lax.rem(z + (NZ - s if right else s), NZ)
                    wait_bytes(zpart(half, b), z_recv.at[0 if right else 1, s - 1, half])
                    if s < 3 or (s == 3 and half == (0 if right else 1)):
                        zhop(s, right, half).start()
        for b in group(s):
            spread(b)

    def group(s):
        if s in (0, 4):
            return [lax.rem(z + s, NZ)]
        return [lax.rem(z + NZ - s, NZ), lax.rem(z + s, NZ)]

    advance(1)
    wait_bytes(pbuf.at[1 - core], prompt_sems.at[4])
    prompt_rows = pbuf[...].reshape(-1, pbuf.shape[-1])
    own_rows = kvbuf[...].reshape(2 * tokens, kvbuf.shape[-1])
    held = prompt_rows.shape[0]
    for g in range(KEY_VALUE_HEADS):
        low, high = g * HEAD_SIZE, (KEY_VALUE_HEADS + g) * HEAD_SIZE
        kcat[g, :held, :] = prompt_rows[:, low : low + HEAD_SIZE]
        kcat[g, held:, :] = own_rows[:, low : low + HEAD_SIZE]
        vcat[g, :held, :] = prompt_rows[:, high : high + HEAD_SIZE]
        vcat[g, held:, :] = own_rows[:, high : high + HEAD_SIZE]

    def attend(j, carry):
        g = lax.div(j, 8)
        first_col = pl.ds(pl.multiple_of(j * 2 * HEAD_SIZE, 128), HEAD_SIZE)
        second_col = pl.ds(pl.multiple_of(j * 2 * HEAD_SIZE + HEAD_SIZE, 128), HEAD_SIZE)
        query = jnp.concatenate([q_ref[:, first_col], q_ref[:, second_col]], axis=0)
        scores = lax.dot_general(
            query, kcat[g], (((1,), (1,)), ((), ())), preferred_element_type=jnp.float32
        )
        scores = scores * (HEAD_SIZE**-0.5) + jnp.concatenate([bias_ref[...], bias_ref[...]], axis=0)
        raised = jnp.exp(scores - jnp.max(scores, axis=1, keepdims=True))
        denom = jnp.sum(raised, axis=1, keepdims=True)
        mixed = jnp.dot(raised.astype(jnp.bfloat16), vcat[g], preferred_element_type=jnp.float32)
        mixed = (mixed / denom).astype(jnp.bfloat16)
        ctx[core, :, first_col] = mixed[:tokens]
        ctx[core, :, second_col] = mixed[tokens:]
        return carry

    pairs = QUERY_HEADS // 2
    lax.fori_loop(0, pairs // 2, attend, 0)
    advance(2)
    relay(group(0)[0])
    lax.fori_loop(pairs // 2, pairs, attend, 0)
    ctx_copy = remote(ctx.at[core], ctx.at[core], ctx_sems.at[0], ctx_sems.at[1], sibling)
    ctx_copy.start()
    for b in group(1):
        relay(b)
    advance(3)
    for b in group(2):
        relay(b)
    advance(4)
    for b in group(3):
        relay(b)
    wait_bytes(ctx.at[1 - core], ctx_sems.at[1])

    def project(b):
        settle(b)

        def part(i, total):
            cols = pl.ds(pl.multiple_of(i * 1024, 1024), 1024)
            left = jnp.concatenate([ctx[0, :, cols], ctx[1, :, cols]], axis=0)
            right = jnp.concatenate([wc[b, 0, i].reshape(1024, 128), wc[b, 1, i].reshape(1024, 128)], axis=1)
            return total + jnp.dot(left, right, preferred_element_type=jnp.float32)

        total = lax.fori_loop(0, NX, part, jnp.zeros((2 * tokens, 256), jnp.float32))
        first_core = core == 0
        own_out[b] = jnp.where(first_core, total[:tokens], total[tokens:])
        send_out[b] = jnp.where(first_core, total[tokens:], total[:tokens])
        remote(send_out.at[b], recv_out.at[b], out_send.at[b], out_recv.at[b], sibling).start()

    def project_early(j, carry):
        near = lax.div(j + 1, 2)
        project(lax.rem(jnp.where(lax.rem(j, 2) == 1, z + NZ - near, z + near), NZ))
        return carry

    lax.fori_loop(0, 5, project_early, 0)
    relay(group(4)[0])
    lax.fori_loop(5, 8, project_early, 0)

    def add_up(b, square):
        wait_bytes(recv_out.at[b], out_recv.at[b])
        for lo in range(2):
            for who, out in ((core, own_out), (1 - core, recv_out)):
                cols = pl.ds(pl.multiple_of(((b * 2 + lo) * 2 + who) * 128, 128), 128)
                summed = hidden_ref[:, cols].astype(jnp.float32) + out[b, :, lo * 128 : (lo + 1) * 128]
                rounded = summed.astype(jnp.bfloat16)
                resid_ref[:, cols] = rounded
                wide = rounded.astype(jnp.float32)
                square = square + wide * wide
        return square

    square = lax.fori_loop(0, NZ, add_up, jnp.zeros((tokens, 128), jnp.float32))
    model = hidden_ref.shape[1]
    scale = lax.rsqrt(jnp.sum(square, axis=1, keepdims=True) * (1.0 / model) + eps_norm)

    def normalise(i, logits):
        cols = pl.ds(pl.multiple_of(i * 512, 512), 512)
        part = (resid_ref[:, cols].astype(jnp.float32) * scale * gain_ref[:, cols]).astype(jnp.bfloat16)
        normed_ref[:, cols] = part
        return logits + jnp.dot(part, router_ref[cols, :], preferred_element_type=jnp.float32)

    logits = lax.fori_loop(0, model // 512, normalise, jnp.zeros((tokens, 128), jnp.float32))
    ranks = ranks_ref[...]
    named = ranks.astype(jnp.float32) > 0.0
    masked = jnp.where(named, logits, neg_fill)
    raised = jnp.where(named, jnp.exp(masked - jnp.max(masked, axis=1, keepdims=True)), 0.0)
    rw_ref[:, :128] = ranks
    rw_ref[:, 128:] = (raised / jnp.sum(raised, axis=1, keepdims=True)).astype(jnp.bfloat16)

    kv_copy.wait_send()
    wait_bytes(pbuf.at[0, 0, pl.ds(0, NZ - 1)], prompt_sems.at[0])
    prompt_pair.wait_send()
    prompt_sib.wait_send()
    wait_bytes(wc.at[0, 0, pl.ds(0, 3), :, 0], first_send.at[0])
    wait_bytes(wc.at[pl.ds(0, NZ - 1), 0, :, :, 0], z_send.at[0])
    ctx_copy.wait_send()

    def drain(b, carry):
        wait_bytes(wc.at[b, :, pl.ds(0, 3)], spread_send.at[b])
        wait_bytes(send_out.at[b], out_send.at[b])
        return carry

    lax.fori_loop(0, NZ, drain, 0)


def attend_all(queries, key_value, prompt, bias, out_weight, hidden, gain, router, ranks):
    tokens, model = queries.shape
    vmem = pl.BlockSpec(memory_space=pltpu.VMEM)
    dma = pltpu.SemaphoreType.DMA
    kv_width = key_value.shape[1]
    keys = bias.shape[1]
    return pl.pallas_call(
        attend_kernel,
        out_shape=(
            jax.ShapeDtypeStruct((tokens, model), jnp.bfloat16),
            jax.ShapeDtypeStruct((tokens, model), jnp.bfloat16),
            jax.ShapeDtypeStruct((tokens, 256), jnp.bfloat16),
        ),
        in_specs=[vmem] * 9,
        out_specs=[vmem] * 3,
        scratch_shapes=[
            pltpu.VMEM((NZ, 2, NX, 2, 2, 256, 128), jnp.bfloat16),
            pltpu.VMEM((2, 2, NZ, prompt.shape[0], kv_width), jnp.bfloat16),
            pltpu.VMEM((2, tokens, kv_width), jnp.bfloat16),
            pltpu.VMEM((KEY_VALUE_HEADS, keys, HEAD_SIZE), jnp.bfloat16),
            pltpu.VMEM((KEY_VALUE_HEADS, keys, HEAD_SIZE), jnp.bfloat16),
            pltpu.VMEM((2, tokens, model), jnp.bfloat16),
            pltpu.VMEM((NZ, tokens, 256), jnp.float32),
            pltpu.VMEM((NZ, tokens, 256), jnp.float32),
            pltpu.VMEM((NZ, tokens, 256), jnp.float32),
            dma((4,)),
            dma((4,)),
            dma((5,)),
            dma((2,)),
            dma((2, 3)),
            dma((1,)),
            dma((2, 4, 2)),
            dma((1,)),
            dma((NZ,)),
            dma((NZ, 2)),
            dma((NZ, 2)),
            dma((NZ, 2)),
            dma((NZ, 2)),
            dma((2,)),
            dma((NZ,)),
            dma((NZ,)),
        ],
        compiler_params=pltpu.CompilerParams(
            collective_id=2, has_side_effects=True, vmem_limit_bytes=56 * 1024 * 1024
        ),
        cost_estimate=pl.CostEstimate(
            flops=2 * tokens * model * (model + 2 * keys), bytes_accessed=8 * tokens * model, transcendentals=0
        ),
        name="attend",
    )(queries, key_value, prompt, bias, out_weight, hidden, gain, router, ranks)


def local(
    hidden,
    queries,
    response_key_value,
    prompt_kv,
    lengths,
    out_weight,
    norm_gain,
    router,
    gate_up,
    routes,
):
    tokens = queries.shape[1]
    exp_index = lax.axis_index("exp")
    core, response = exp_index % 2, exp_index // 2
    length_now = lax.dynamic_index_in_dim(lengths[0], response, 0, keepdims=False)
    step_ids = jnp.arange(tokens, dtype=jnp.int32)
    query_pos = core * tokens + step_ids
    key_pos = jnp.arange(2 * tokens, dtype=jnp.int32)
    own_allowed = (key_pos[None, :] <= query_pos[:, None]) & (key_pos < length_now)[None, :]
    prompt_rows = prompt_kv.shape[1]
    held_rows = -(-prompt_rows // 16) * 16
    prompt_place = jnp.arange(lax.axis_size("exp") * held_rows, dtype=jnp.int32) % held_rows
    prompt_allowed = jnp.broadcast_to(
        (prompt_place < prompt_rows)[None, :], (tokens, prompt_place.shape[0])
    )
    bias = jnp.where(
        jnp.concatenate([prompt_allowed, own_allowed], axis=1), jnp.float32(0), jnp.float32(neg_fill)
    )
    prompt = jnp.pad(prompt_kv[0], ((0, held_rows - prompt_rows), (0, 0)))
    experts = router.shape[1]
    named = jnp.any(
        routes[0][:, :, None] == jnp.arange(experts, dtype=jnp.int32)[None, None, :], axis=1
    )
    earlier = step_ids[:, None] >= step_ids[None, :]
    ranks = jnp.dot(
        earlier.astype(jnp.bfloat16), named.astype(jnp.bfloat16), preferred_element_type=jnp.float32
    )
    ranks = jnp.where(named, ranks, 0.0).astype(jnp.bfloat16)
    resid_out, normed, rank_weight = attend_all(
        queries[0],
        response_key_value[0],
        prompt,
        bias,
        out_weight,
        hidden[0],
        norm_gain[None, :],
        router,
        ranks,
    )
    slots = dispatch(normed, rank_weight, gate_up[0])
    expert_act = (
        slots.reshape(2, NX, 2, 2, NZ, CAP, -1)
        .transpose(1, 2, 4, 3, 0, 5, 6)
        .reshape(1, 2 * NX * NZ * NY, CAP, -1)
    )
    return (resid_out[None], expert_act)


def solution(mesh):
    placed = (
        P("grp", "exp", None),
        P("grp", "exp", None),
        P("grp", "exp", None),
        P("grp", "exp", None),
        P("grp", None),
        P("grp", "exp"),
        P(),
        P(),
        P(("grp", "exp"), None, None),
        P("grp", "exp", None),
    )
    return jax.shard_map(
        local,
        mesh=mesh,
        in_specs=placed,
        out_specs=(P("grp", "exp", None), P(("grp", "exp"), None, None, None)),
        check_vma=False,
    )
```

```python
import functools

import jax
import jax.numpy as jnp
from jax import lax
from jax.experimental import pallas as pl
from jax.experimental.pallas import tpu as pltpu
from jax.sharding import PartitionSpec as P

QUERY_HEADS = 32
KEY_VALUE_HEADS = 2
HEAD_SIZE = 128


neg_fill = -1e30
eps_norm = 1e-06


MESH = pl.DeviceIdType.MESH
NX, NY, NZ, NYL = 4, 4, 8, 2
CHUNKS = 16
CAP = 6
PEERS = NX * NY
PEER_ROWS = NZ * CAP
COLUMN_ROWS = NY * PEER_ROWS
SLOT_ROWS = PEERS * PEER_ROWS
SECOND_LAG = 2
MULTIPLY_LAG = 4


def position():
    g, i = lax.axis_index("grp"), lax.axis_index("exp")
    x, y_hi = lax.div(g, 2), lax.rem(g, 2)
    z, y_lo, core = lax.div(i, 4), lax.rem(lax.div(i, 2), 2), lax.rem(i, 2)
    return x, y_hi * 2 + y_lo, z, core


def device(x, y, z, core):
    return (x * 2 + lax.div(y, 2), (z * 2 + lax.rem(y, 2)) * 2 + core)


def remote(src, dst, send, recv, to):
    return pltpu.make_async_remote_copy(
        src_ref=src, dst_ref=dst, send_sem=send, recv_sem=recv, device_id=to, device_id_type=MESH
    )


def wait_bytes(ref, sem):
    pltpu.make_async_copy(ref, ref, sem).wait()


def plane_expert(rows, z):
    row = lax.broadcasted_iota(jnp.int32, (rows, 1), 0).astype(jnp.float32)
    place = jnp.floor((row + 0.5) * (1.0 / PEER_ROWS))
    within = row - place * PEER_ROWS
    source = jnp.floor((within + 0.5) * (1.0 / CAP))
    slot = within - source * CAP
    px = jnp.floor((place + 0.5) * (1.0 / NY))
    py = place - px * NY
    py_hi = jnp.floor((py + 0.5) * 0.5)
    expert = px * (4 * NZ) + py_hi * (2 * NZ) + (py - py_hi * 2) + (z * 2).astype(jnp.float32)
    lane = lax.broadcasted_iota(jnp.int32, (rows, 128), 1).astype(jnp.float32)
    return lane == expert, source, slot


def dispatch_kernel(
    x_ref,
    weight_ref,
    sel,
    gu_ref,
    out_ref,
    xall,
    weights,
    wbuf,
    sendb,
    mid,
    recvb,
    wsend,
    wmid,
    wrecv,
    acc,
    outsend,
    z_right,
    z_left,
    z_send,
    weight_right,
    weight_left,
    weight_send,
    x_send,
    x_recv,
    y_send,
    y_recv,
    w_sems,
    gu_sems,
    out_sems,
):
    x, y, z, core = position()
    up, down = lax.rem(z + 1, NZ), lax.rem(z + NZ - 1, NZ)
    up_dev, down_dev = device(x, y, up, core), device(x, y, down, core)
    sibling = device(x, y, z, 1 - core)
    xs = [lax.rem(x + d, NX) for d in range(NX)]
    ys = [lax.rem(y + d, NY) for d in range(NY)]
    x_dev = [device(xs[d], y, z, core) for d in range(NX)]
    y_dev = [device(x, ys[d], z, core) for d in range(NY)]
    width = x_ref.shape[1] // CHUNKS
    order = (2, 1, 3)

    barrier = pltpu.get_barrier_semaphore()
    partners = x_dev[1:] + y_dev[1:] + [up_dev, down_dev, sibling]
    for to in partners:
        pl.semaphore_signal(barrier, inc=1, device_id=to, device_id_type=MESH)
    pl.semaphore_wait(barrier, len(partners))

    def weight_hop(step, right):
        if right:
            block, to, sem = lax.rem(z + NZ - step, NZ), up_dev, weight_right
        else:
            block, to, sem = lax.rem(z + step, NZ), down_dev, weight_left
        return remote(weights.at[block], weights.at[block], weight_send.at[0], sem.at[step], to)

    def hop(k, step, right):
        if right:
            block, to, sem = lax.rem(z + NZ - step, NZ), up_dev, z_right
        else:
            block, to, sem = lax.rem(z + step, NZ), down_dev, z_left
        return remote(xall.at[k, block], xall.at[k, block], z_send.at[k], sem.at[k, step], to)

    def along_x(src, dst, send, recv):
        for d in order:
            remote(src.at[xs[d]], dst.at[x], send, recv, x_dev[d]).start()

    def along_y(src, dst, send, recv):
        for d in order:
            remote(src.at[:, ys[d]], dst.at[y], send, recv, y_dev[d]).start()

    own_copy = pltpu.make_async_copy(gu_ref, wbuf.at[core], gu_sems.at[0])
    other_copy = remote(gu_ref, wbuf.at[core], gu_sems.at[1], gu_sems.at[2], sibling)
    for k in range(CHUNKS):
        xall[k, z] = x_ref[:, k * width : (k + 1) * width]
        if k < 2:
            hop(k, 0, True).start()
            hop(k, 0, False).start()
        if k == 2:
            weights[z] = weight_ref[...]
            weight_hop(0, True).start()
            weight_hop(0, False).start()
            own_copy.start()
            other_copy.start()

    def zero(r, carry):
        rows = pl.ds(pl.multiple_of(lax.rem(r, NX) * COLUMN_ROWS, COLUMN_ROWS), COLUMN_ROWS)
        acc[lax.div(r, NX), rows, :] = jnp.zeros((COLUMN_ROWS, acc.shape[2]), jnp.float32)
        return carry

    lax.fori_loop(0, 2 * NX, zero, 0)

    def tick(t, carry):
        for step in (4, 3, 2, 1):
            k = t - step

            @pl.when((k >= 0) & (k < CHUNKS))
            def _():
                even = lax.rem(k, 2) == 0
                if step == 4:

                    @pl.when(even)
                    def _():
                        hop(k, 3, True).wait_recv()

                    @pl.when(jnp.logical_not(even))
                    def _():
                        hop(k, 3, False).wait_recv()
                else:
                    hop(k, step - 1, True).wait_recv()
                    if step < 3:
                        hop(k, step, True).start()
                    else:

                        @pl.when(even)
                        def _():
                            hop(k, step, True).start()

                    hop(k, step - 1, False).wait_recv()
                    if step < 3:
                        hop(k, step, False).start()
                    else:

                        @pl.when(jnp.logical_not(even))
                        def _():
                            hop(k, step, False).start()

        @pl.when(t + 2 < CHUNKS)
        def _():
            hop(t + 2, 0, True).start()
            hop(t + 2, 0, False).start()

        @pl.when((t >= 1) & (t <= 4))
        def _():
            weight_hop(t - 1, True).wait_recv()

            @pl.when(t < 4)
            def _():
                weight_hop(t - 1, False).wait_recv()
                weight_hop(t, True).start()

            @pl.when(t < 3)
            def _():
                weight_hop(t, False).start()

        k_sel = t - 4

        @pl.when((k_sel >= 0) & (k_sel < CHUNKS))
        def _():
            picked = jnp.dot(
                sel[...], xall[k_sel].reshape(-1, width), preferred_element_type=jnp.float32
            )
            sendb[k_sel] = picked.astype(jnp.bfloat16).reshape(NX, NY, PEER_ROWS, width)
            along_x(sendb.at[k_sel], mid.at[k_sel], x_send.at[k_sel], x_recv.at[k_sel])
            mid[k_sel, x] = sendb[k_sel, x]

        @pl.when(t == 6)
        def _():
            chosen, _, _ = plane_expert(SLOT_ROWS, z)
            spread = jnp.dot(
                sel[...], weights[...].reshape(-1, weights.shape[2]), preferred_element_type=jnp.float32
            )
            column = jnp.sum(jnp.where(chosen, spread, 0.0), axis=1, keepdims=True)
            wsend[...] = (
                jnp.broadcast_to(column, (SLOT_ROWS, 128)).astype(jnp.bfloat16).reshape(wsend.shape)
            )
            along_x(wsend, wmid, w_sems.at[0], w_sems.at[1])
            wmid[x] = wsend[x]

        @pl.when(t == 9)
        def _():
            wait_bytes(wmid.at[pl.ds(0, NX - 1)], w_sems.at[1])
            along_y(wmid, wrecv, w_sems.at[2], w_sems.at[3])
            wrecv[y] = wmid[:, y]

        k_mid = t - 4 - SECOND_LAG

        @pl.when((k_mid >= 0) & (k_mid < CHUNKS))
        def _():
            wait_bytes(mid.at[k_mid, pl.ds(0, NX - 1)], x_recv.at[k_mid])
            along_y(mid.at[k_mid], recvb.at[k_mid], y_send.at[k_mid], y_recv.at[k_mid])
            recvb[k_mid, y] = mid[k_mid, :, y]

        k_mul = t - 4 - MULTIPLY_LAG

        @pl.when(k_mul >= 0)
        def _():
            @pl.when(k_mul == 0)
            def _():
                own_copy.wait()
                other_copy.wait_recv()

            wait_bytes(recvb.at[k_mul, pl.ds(0, NY - 1)], y_recv.at[k_mul])
            cols = pl.ds(pl.multiple_of(k_mul * width, width), width)

            def multiply(r, c):
                h = lax.div(r, 3)
                inner = pl.ds(pl.multiple_of(lax.rem(r, 3) * 256, 256), 256)
                acc[h, :, inner] += jnp.dot(
                    recvb[k_mul].reshape(SLOT_ROWS, width),
                    wbuf[h, cols, inner],
                    preferred_element_type=jnp.float32,
                )
                return c

            lax.fori_loop(0, 6, multiply, 0)

        return carry

    lax.fori_loop(0, CHUNKS + 4 + MULTIPLY_LAG, tick, 0)

    wait_bytes(wrecv.at[pl.ds(0, NY - 1)], w_sems.at[3])
    half = acc.shape[2] // 2

    def finish(h, part):
        rows = pl.ds(pl.multiple_of(part * COLUMN_ROWS, COLUMN_ROWS), COLUMN_ROWS)
        gate, lift = acc[h, rows, :half], acc[h, rows, half:]
        weight = wrecv[part].reshape(COLUMN_ROWS, 128)[:, :1].astype(jnp.float32)
        return rows, (weight * (gate / (1.0 + jnp.exp(-gate))) * lift).astype(jnp.bfloat16)

    def finish_other(part, c):
        rows, values = finish(1 - core, part)
        outsend[rows, :] = values
        return c

    def finish_own(part, c):
        rows, values = finish(core, part)
        out_ref[core, rows, :] = values
        return c

    lax.fori_loop(0, NY, finish_other, 0)
    out_copy = remote(outsend, out_ref.at[core], out_sems.at[0], out_sems.at[1], sibling)
    out_copy.start()
    lax.fori_loop(0, NY, finish_own, 0)

    def drain(k, c):
        wait_bytes(xall.at[k, pl.ds(0, NZ - 1)], z_send.at[k])
        wait_bytes(sendb.at[k, pl.ds(0, NX - 1)], x_send.at[k])
        wait_bytes(mid.at[k, pl.ds(0, NX - 1)], y_send.at[k])
        return c

    lax.fori_loop(0, CHUNKS, drain, 0)
    wait_bytes(weights.at[pl.ds(0, NZ - 1)], weight_send.at[0])
    wait_bytes(wsend.at[pl.ds(0, NX - 1)], w_sems.at[0])
    wait_bytes(wmid.at[pl.ds(0, NX - 1)], w_sems.at[2])
    other_copy.wait_send()
    out_copy.wait()


def dispatch(normed, weight, sel, gate_up):
    tokens, model = normed.shape
    width = model // CHUNKS
    inner = gate_up.shape[1]
    vmem = pl.BlockSpec(memory_space=pltpu.VMEM)
    dma = pltpu.SemaphoreType.DMA
    rows = (NX, NY, PEER_ROWS)
    return pl.pallas_call(
        dispatch_kernel,
        out_shape=jax.ShapeDtypeStruct((2, SLOT_ROWS, inner // 2), jnp.bfloat16),
        in_specs=[vmem, vmem, vmem, pl.BlockSpec(memory_space=pl.ANY)],
        out_specs=vmem,
        scratch_shapes=[
            pltpu.VMEM((CHUNKS, NZ, tokens, width), jnp.bfloat16),
            pltpu.VMEM((NZ, tokens, 128), jnp.bfloat16),
            pltpu.VMEM((2, model, inner), jnp.bfloat16),
            pltpu.VMEM((CHUNKS, *rows, width), jnp.bfloat16),
            pltpu.VMEM((CHUNKS, *rows, width), jnp.bfloat16),
            pltpu.VMEM((CHUNKS, *rows, width), jnp.bfloat16),
            pltpu.VMEM((*rows, 128), jnp.bfloat16),
            pltpu.VMEM((*rows, 128), jnp.bfloat16),
            pltpu.VMEM((*rows, 128), jnp.bfloat16),
            pltpu.VMEM((2, SLOT_ROWS, inner), jnp.float32),
            pltpu.VMEM((SLOT_ROWS, inner // 2), jnp.bfloat16),
            dma((CHUNKS, 4)),
            dma((CHUNKS, 4)),
            dma((CHUNKS,)),
            dma((4,)),
            dma((4,)),
            dma((1,)),
            dma((CHUNKS,)),
            dma((CHUNKS,)),
            dma((CHUNKS,)),
            dma((CHUNKS,)),
            dma((4,)),
            dma((3,)),
            dma((2,)),
        ],
        compiler_params=pltpu.CompilerParams(
            collective_id=1, has_side_effects=True, vmem_limit_bytes=62 * 1024 * 1024
        ),
        cost_estimate=pl.CostEstimate(
            flops=2 * SLOT_ROWS * model * (2 * inner + NZ * tokens),
            bytes_accessed=model * inner * 2,
            transcendentals=0,
        ),
        name="dispatch",
    )(normed, weight, sel, gate_up)


def attend_kernel(
    prompt_rows,
    q_hbm,
    kv_ref,
    prompt_ref,
    lengths_ref,
    w_hbm,
    hidden_hbm,
    gain_ref,
    router_hbm,
    routes_ref,
    resid_ref,
    normed_ref,
    weight_ref,
    sel_ref,
    q_ref,
    hidden_ref,
    router_ref,
    bias_ref,
    ranks,
    wc,
    pbuf,
    kvbuf,
    kcat,
    vcat,
    ctx,
    send_out,
    recv_out,
    load_sems,
    rank_sems,
    prompt_sems,
    kv_sems,
    z_recv,
    z_send,
    near_recv,
    spread_send,
    x_direct,
    x_relay,
    y_direct,
    y_relay,
    ctx_send,
    ctx_recv,
    out_send,
    out_recv,
):
    x, y, z, core = position()
    y_hi, y_lo = lax.div(y, 2), lax.rem(y, 2)
    z_pair, z_side = lax.div(z, 2), lax.rem(z, 2)
    xs = [lax.rem(x + d, NX) for d in range(NX)]
    ys = [lax.rem(y + d, NY) for d in range(NY)]
    x_dev = [device(xs[d], y, z, core) for d in range(NX)]
    y_dev = [device(x, ys[d], z, core) for d in range(NY)]
    z_dev = [device(x, y, lax.rem(z + d, NZ), core) for d in range(NZ)]
    sibling = device(x, y, z, 1 - core)
    twin = device(x, y, z_pair * 2 + 1 - z_side, core)
    cross = device(x, y, z_pair * 2 + 1 - z_side, 1 - core)
    pair_dev = device(x, y_hi * 2 + 1 - y_lo, z, core)

    barrier = pltpu.get_barrier_semaphore()
    partners = x_dev[1:] + y_dev[1:] + z_dev[1:] + [sibling, cross]
    for to in partners:
        pl.semaphore_signal(barrier, inc=1, device_id=to, device_id_type=MESH)
    pl.semaphore_wait(barrier, len(partners))

    steps = NZ // 2
    chunks = [lax.rem(z_pair + d, steps) for d in (0, 1, 3, 2)]

    def own_shard(half):
        return w_hbm.at[pl.ds(half * 256, 256)]

    def near(j, half, d, src):
        part = wc.at[j, y_lo, x, y_hi, half]
        to = (y_dev, x_dev)[half][d]
        remote(src, part, spread_send.at[j, 1], near_recv.at[j, half, d - 1], to).start()

    def xpart(j, d):
        return wc.at[j, :, xs[d], :, 0]

    def ypart(j, d):
        return wc.at[j, lax.rem(ys[d], 2), :, lax.div(ys[d], 2), 1]

    def xhalf(j, d, which):
        return wc.at[j, :, xs[d], which, 0]

    def yhalf(j, d, which):
        return wc.at[j, lax.rem(ys[d], 2), pl.ds(2 * which, 2), lax.div(ys[d], 2), 1]

    def begin(j):
        for d in (1, 3, 2):
            for half in range(2):
                near(j, half, d, wc.at[j, y_lo, x, y_hi, half])

    def spread(j):
        for half in range(2):
            for d in (1, 3, 2):
                if half == 0:
                    part = wc.at[j, lax.rem(ys[4 - d], 2), x, lax.div(ys[4 - d], 2), 0]
                else:
                    part = wc.at[j, y_lo, xs[4 - d], y_hi, 1]
                wait_bytes(part, near_recv.at[j, half, d - 1])
            parts, devs, sem = ((xpart, x_dev, x_direct), (ypart, y_dev, y_direct))[half]
            part = parts(j, 0)
            remote(part, part, spread_send.at[j, 0], sem.at[j, 0], devs[1]).start()
            remote(part, part, spread_send.at[j, 0], sem.at[j, 1], devs[3]).start()

    def relay(j):
        for parts, halves, devs, sem, next_sem in (
            (xpart, xhalf, x_dev, x_direct, x_relay),
            (ypart, yhalf, y_dev, y_direct, y_relay),
        ):
            wait_bytes(parts(j, 3), sem.at[j, 0])
            part = halves(j, 3, 0)
            remote(part, part, spread_send.at[j, 0], next_sem.at[j, 0], devs[1]).start()
            wait_bytes(parts(j, 1), sem.at[j, 1])
            part = halves(j, 1, 1)
            remote(part, part, spread_send.at[j, 0], next_sem.at[j, 1], devs[3]).start()

    def settle(j):
        for halves, next_sem in ((xhalf, x_relay), (yhalf, y_relay)):
            for which in range(2):
                wait_bytes(halves(j, 2, which), next_sem.at[j, which])

    tokens = kv_ref.shape[0]
    for d in (1, 3, 2):
        for half in range(2):
            near(z_pair, half, d, own_shard(half))
    own_weight = [
        pltpu.make_async_copy(own_shard(half), wc.at[z_pair, y_lo, x, y_hi, half], load_sems.at[half])
        for half in range(2)
    ]
    for copy in own_weight:
        copy.start()
    pbuf[core, y_lo, z] = prompt_ref[...]
    for d in (4, 3, 5, 2, 6, 1, 7):
        part = pbuf.at[core, y_lo, z]
        remote(part, part, prompt_sems.at[0], prompt_sems.at[5], z_dev[d]).start()
    for d in (1, 3, 2):
        for half in range(2):
            part = wc.at[z_pair, y_lo, x, y_hi, half]
            remote(own_shard(half), part, z_send.at[0], z_recv.at[half, d - 1], z_dev[2 * d]).start()
    kv_copy = remote(kv_ref, kvbuf.at[core], kv_sems.at[0], kv_sems.at[1], sibling)
    kv_copy.start()
    loads = [
        pltpu.make_async_copy(src, dst, load_sems.at[2 + i])
        for i, (src, dst) in enumerate(((q_hbm, q_ref), (hidden_hbm, hidden_ref), (router_hbm, router_ref)))
    ]
    for copy in loads:
        copy.start()
    kvbuf[core] = kv_ref[...]

    wait_bytes(pbuf.at[core, y_lo, pl.ds(0, NZ - 1)], prompt_sems.at[5])
    part = pbuf.at[core, y_lo]
    prompt_pair = remote(part, part, prompt_sems.at[1], prompt_sems.at[2], pair_dev)
    prompt_pair.start()
    for copy in own_weight:
        copy.wait()
    spread(chunks[0])

    lane = lax.broadcasted_iota(jnp.int32, (tokens, 128), 1)
    row = lax.broadcasted_iota(jnp.int32, (tokens, 128), 0)
    named = routes_ref[:, 0:1] == lane
    for k in range(1, routes_ref.shape[1]):
        named = named | (routes_ref[:, k : k + 1] == lane)
    earlier = jnp.where(row >= lane, 1.0, 0.0).astype(jnp.bfloat16)
    counted = jnp.dot(
        earlier, jnp.where(named, 1.0, 0.0).astype(jnp.bfloat16), preferred_element_type=jnp.float32
    )
    ranks[z] = jnp.where(named, counted, 0.0).astype(jnp.bfloat16)
    for d in (4, 3, 5, 2, 6, 1, 7):
        remote(ranks.at[z], ranks.at[z], rank_sems.at[0], rank_sems.at[1], z_dev[d]).start()

    keys = bias_ref.shape[1]
    held = keys - 2 * tokens
    length = lengths_ref[0, z * 2 + y_lo]
    place = lax.broadcasted_iota(jnp.int32, (tokens, held), 1)
    bias_ref[:, :held] = jnp.where((place & 15) < prompt_rows, 0.0, neg_fill)
    place = lax.broadcasted_iota(jnp.int32, (tokens, 2 * tokens), 1)
    moment = lax.broadcasted_iota(jnp.int32, (tokens, 2 * tokens), 0) + core * tokens
    bias_ref[:, held:] = jnp.where((place <= moment) & (place < length), 0.0, neg_fill)

    wait_bytes(pbuf.at[core, 1 - y_lo], prompt_sems.at[2])
    prompt_sib = remote(pbuf.at[core], pbuf.at[core], prompt_sems.at[3], prompt_sems.at[4], sibling)
    prompt_sib.start()
    for d, j in ((1, chunks[2]), (3, chunks[1]), (2, chunks[3])):
        for half in range(2):
            wait_bytes(wc.at[j, y_lo, x, y_hi, half], z_recv.at[half, d - 1])
        begin(j)
    wait_bytes(kvbuf.at[1 - core], kv_sems.at[1])
    wait_bytes(pbuf.at[1 - core], prompt_sems.at[4])
    prompt_keys = pbuf[...].reshape(-1, pbuf.shape[-1])
    own_rows = kvbuf[...].reshape(2 * tokens, kvbuf.shape[-1])
    for g in range(KEY_VALUE_HEADS):
        low, high = g * HEAD_SIZE, (KEY_VALUE_HEADS + g) * HEAD_SIZE
        kcat[g, :held, :] = prompt_keys[:, low : low + HEAD_SIZE]
        kcat[g, held:, :] = own_rows[:, low : low + HEAD_SIZE]
        vcat[g, :held, :] = prompt_keys[:, high : high + HEAD_SIZE]
        vcat[g, held:, :] = own_rows[:, high : high + HEAD_SIZE]
    loads[0].wait()
    spread(chunks[2])
    relay(chunks[0])
    spread(chunks[1])

    pairs = QUERY_HEADS // 2
    sections = ctx.shape[2]

    def attend(section, i, carry):
        g = section * KEY_VALUE_HEADS // sections
        j = section * (pairs // sections) + i
        query = jnp.concatenate(
            [
                q_ref[:, pl.ds(pl.multiple_of((j * 2 + n) * HEAD_SIZE, HEAD_SIZE), HEAD_SIZE)]
                for n in range(2)
            ],
            axis=0,
        )
        scores = lax.dot_general(
            query, kcat[g], (((1,), (1,)), ((), ())), preferred_element_type=jnp.float32
        )
        scores = scores * (HEAD_SIZE**-0.5) + jnp.concatenate([bias_ref[...], bias_ref[...]], axis=0)
        raised = jnp.exp(scores - jnp.max(scores, axis=1, keepdims=True))
        denom = jnp.sum(raised, axis=1, keepdims=True)
        mixed = jnp.dot(raised.astype(jnp.bfloat16), vcat[g], preferred_element_type=jnp.float32)
        mixed = (mixed / denom).astype(jnp.bfloat16)
        for n in range(2):
            cols = pl.ds(pl.multiple_of((i * 2 + n) * HEAD_SIZE, HEAD_SIZE), HEAD_SIZE)
            ctx[z_side, core, section, :, cols] = mixed[n * tokens : (n + 1) * tokens]
        return carry

    def ctx_move(section, side, to, which):
        part = ctx.at[side, core, section]
        return remote(part, part, ctx_send.at[section, which], ctx_recv.at[section, which], to)

    for section in range(sections):
        lax.fori_loop(0, pairs // sections, functools.partial(attend, section), 0)
        ctx_move(section, z_side, twin, 0).start()
        ctx_move(section, z_side, sibling, 1).start()
        if section == 0:
            relay(chunks[2])
            spread(chunks[3])
    relay(chunks[1])

    wait_bytes(ranks.at[pl.ds(0, NZ - 1)], rank_sems.at[1])
    chosen, source, slot = plane_expert(SLOT_ROWS, z)
    picker = jnp.where(chosen, 1.0, 0.0).astype(jnp.bfloat16)
    for b in range(NZ):
        found = lax.dot_general(
            picker, ranks[b], (((1,), (1,)), ((), ())), preferred_element_type=jnp.float32
        )
        hit = (found == slot + 1.0) & (source == float(b))
        sel_ref[:, b * tokens : (b + 1) * tokens] = jnp.where(hit, 1.0, 0.0).astype(jnp.bfloat16)

    relay(chunks[3])
    for section in range(sections):
        wait_bytes(ctx.at[1 - z_side, core, section], ctx_recv.at[section, 0])
        ctx_move(section, 1 - z_side, sibling, 2).start()
    for section in range(sections):
        wait_bytes(ctx.at[z_side, 1 - core, section], ctx_recv.at[section, 1])
        wait_bytes(ctx.at[1 - z_side, 1 - core, section], ctx_recv.at[section, 2])

    def out_move(j, side, who, to, which):
        return remote(
            send_out.at[j, side, who],
            recv_out.at[z_side, core, j],
            out_send.at[j, which],
            out_recv.at[j, which],
            to,
        )

    def out_moves(j):
        return (
            out_move(j, 1 - z_side, core, twin, 0),
            out_move(j, 1 - z_side, 1 - core, cross, 1),
            out_move(j, z_side, 1 - core, sibling, 2),
        )

    deep = 4096 // NX

    def project(j):
        settle(j)

        def part(i, total):
            cols = pl.ds(pl.multiple_of(lax.rem(i, 2) * deep, deep), deep)
            left = ctx[:, :, lax.div(i, 2), :, cols].reshape(4 * tokens, deep)
            right = jnp.concatenate(
                [wc[j, 0, i].reshape(deep, 128), wc[j, 1, i].reshape(deep, 128)], axis=1
            )
            return total + jnp.dot(left, right, preferred_element_type=jnp.float32)

        total = lax.fori_loop(0, NX, part, jnp.zeros((4 * tokens, 256), jnp.float32))
        send_out[j] = total.astype(jnp.bfloat16).reshape(2, 2, tokens, 256)
        for move in out_moves(j):
            move.start()
        recv_out[z_side, core, j] = send_out[j, z_side, core]

    def chunk_at(i):
        d = jnp.where(i == 1, 3, jnp.where(i == 2, 1, jnp.where(i == 3, 2, 0)))
        return lax.rem(z_pair + d, steps)

    def project_at(i, carry):
        project(chunk_at(i))
        return carry

    def add_up(i, square):
        j = chunk_at(i)
        wait_bytes(recv_out.at[1 - z_side, core, j], out_recv.at[j, 0])
        wait_bytes(recv_out.at[1 - z_side, 1 - core, j], out_recv.at[j, 1])
        wait_bytes(recv_out.at[z_side, 1 - core, j], out_recv.at[j, 2])
        for side in range(2):
            for lo in range(2):
                for who in range(2):
                    cols = pl.ds(pl.multiple_of((((j * 2 + side) * 2 + lo) * 2 + who) * 128, 128), 128)
                    part = recv_out[side, who, j, :, lo * 128 : (lo + 1) * 128].astype(jnp.float32)
                    rounded = (hidden_ref[:, cols].astype(jnp.float32) + part).astype(jnp.bfloat16)
                    resid_ref[:, cols] = rounded
                    wide = rounded.astype(jnp.float32)
                    square = square + wide * wide
        return square

    lax.fori_loop(0, steps, project_at, 0)
    loads[1].wait()
    loads[2].wait()
    square = lax.fori_loop(0, steps, add_up, jnp.zeros((tokens, 128), jnp.float32))
    model = hidden_ref.shape[1]
    scale = lax.rsqrt(jnp.sum(square, axis=1, keepdims=True) * (1.0 / model) + eps_norm)

    def normalise(i, logits):
        cols = pl.ds(pl.multiple_of(i * 512, 512), 512)
        part = (resid_ref[:, cols].astype(jnp.float32) * scale * gain_ref[:, cols]).astype(jnp.bfloat16)
        normed_ref[:, cols] = part
        return logits + jnp.dot(part, router_ref[cols, :], preferred_element_type=jnp.float32)

    logits = lax.fori_loop(0, model // 512, normalise, jnp.zeros((tokens, 128), jnp.float32))
    named = ranks[z].astype(jnp.float32) > 0.0
    masked = jnp.where(named, logits, neg_fill)
    raised = jnp.where(named, jnp.exp(masked - jnp.max(masked, axis=1, keepdims=True)), 0.0)
    weight_ref[...] = (raised / jnp.sum(raised, axis=1, keepdims=True)).astype(jnp.bfloat16)

    kv_copy.wait_send()
    wait_bytes(ranks.at[pl.ds(0, NZ - 1)], rank_sems.at[0])
    wait_bytes(pbuf.at[0, 0, pl.ds(0, NZ - 1)], prompt_sems.at[0])
    prompt_pair.wait_send()
    prompt_sib.wait_send()
    wait_bytes(wc.at[0, 0, pl.ds(0, 3), :, 0], z_send.at[0])
    for section in range(sections):
        for which in range(3):
            wait_bytes(ctx.at[z_side, core, section], ctx_send.at[section, which])

    def drain(j, carry):
        wait_bytes(wc.at[j, :, pl.ds(0, 3)], spread_send.at[j, 0])
        wait_bytes(wc.at[j, 0, pl.ds(0, 3), :, 0], spread_send.at[j, 1])
        for move in out_moves(j):
            move.wait_send()
        return carry

    lax.fori_loop(0, steps, drain, 0)


def attend_all(queries, key_value, prompt, prompt_rows, lengths, out_weight, hidden, gain, router, routes):
    tokens, model = queries.shape
    vmem, hbm = pl.BlockSpec(memory_space=pltpu.VMEM), pl.BlockSpec(memory_space=pl.ANY)
    smem = pl.BlockSpec(memory_space=pltpu.SMEM)
    dma = pltpu.SemaphoreType.DMA
    kv_width = key_value.shape[1]
    keys = 2 * NYL * NZ * prompt.shape[0] + 2 * tokens
    experts = router.shape[1]
    return pl.pallas_call(
        functools.partial(attend_kernel, prompt_rows),
        out_shape=(
            jax.ShapeDtypeStruct((tokens, model), jnp.bfloat16),
            jax.ShapeDtypeStruct((tokens, model), jnp.bfloat16),
            jax.ShapeDtypeStruct((tokens, experts), jnp.bfloat16),
            jax.ShapeDtypeStruct((SLOT_ROWS, NZ * tokens), jnp.bfloat16),
        ),
        in_specs=[hbm, vmem, vmem, smem, hbm, hbm, vmem, hbm, vmem],
        out_specs=[vmem] * 4,
        scratch_shapes=[
            pltpu.VMEM((tokens, model), jnp.bfloat16),
            pltpu.VMEM((tokens, model), jnp.bfloat16),
            pltpu.VMEM((model, experts), jnp.bfloat16),
            pltpu.VMEM((tokens, keys), jnp.float32),
            pltpu.VMEM((NZ, tokens, experts), jnp.bfloat16),
            pltpu.VMEM((NZ // 2, 2, NX, 2, 2, 256, 128), jnp.bfloat16),
            pltpu.VMEM((2, 2, NZ, prompt.shape[0], kv_width), jnp.bfloat16),
            pltpu.VMEM((2, tokens, kv_width), jnp.bfloat16),
            pltpu.VMEM((KEY_VALUE_HEADS, keys, HEAD_SIZE), jnp.bfloat16),
            pltpu.VMEM((KEY_VALUE_HEADS, keys, HEAD_SIZE), jnp.bfloat16),
            pltpu.VMEM((2, 2, 2, tokens, model // 2), jnp.bfloat16),
            pltpu.VMEM((NZ // 2, 2, 2, tokens, 256), jnp.bfloat16),
            pltpu.VMEM((2, 2, NZ // 2, tokens, 256), jnp.bfloat16),
            dma((5,)),
            dma((2,)),
            dma((6,)),
            dma((2,)),
            dma((2, 3)),
            dma((1,)),
            dma((NZ // 2, 2, 3)),
            dma((NZ // 2, 2)),
            dma((NZ // 2, 2)),
            dma((NZ // 2, 2)),
            dma((NZ // 2, 2)),
            dma((NZ // 2, 2)),
            dma((2, 3)),
            dma((2, 3)),
            dma((NZ // 2, 3)),
            dma((NZ // 2, 3)),
        ],
        compiler_params=pltpu.CompilerParams(
            collective_id=2, has_side_effects=True, vmem_limit_bytes=62 * 1024 * 1024
        ),
        cost_estimate=pl.CostEstimate(
            flops=2 * tokens * model * (model + 2 * keys), bytes_accessed=8 * tokens * model, transcendentals=0
        ),
        name="attend",
    )(queries, key_value, prompt, lengths, out_weight, hidden, gain, router, routes)


def local(
    hidden,
    queries,
    response_key_value,
    prompt_kv,
    lengths,
    out_weight,
    norm_gain,
    router,
    gate_up,
    routes,
):
    prompt_rows = prompt_kv.shape[1]
    held_rows = -(-prompt_rows // 16) * 16
    prompt = jnp.pad(prompt_kv[0], ((0, held_rows - prompt_rows), (0, 0)))
    resid_out, normed, weight, sel = attend_all(
        queries[0],
        response_key_value[0],
        prompt,
        prompt_rows,
        lengths,
        out_weight,
        hidden[0],
        norm_gain[None, :],
        router,
        routes[0],
    )
    slots = dispatch(normed, weight, sel, gate_up[0])
    expert_act = (
        slots.reshape(2, 2, 2, NX, NZ, CAP, -1)
        .transpose(3, 1, 4, 2, 0, 5, 6)
        .reshape(1, 2 * NX * NZ * NY, CAP, -1)
    )
    return (resid_out[None], expert_act)


def solution(mesh):
    placed = (
        P("grp", "exp", None),
        P("grp", "exp", None),
        P("grp", "exp", None),
        P("grp", "exp", None),
        P("grp", None),
        P("grp", "exp"),
        P(),
        P(),
        P(("grp", "exp"), None, None),
        P("grp", "exp", None),
    )
    return jax.shard_map(
        local,
        mesh=mesh,
        in_specs=placed,
        out_specs=(P("grp", "exp", None), P(("grp", "exp"), None, None, None)),
        check_vma=False,
    )
```

```python
import functools

import jax
import jax.numpy as jnp
from jax import lax
from jax.experimental import pallas as pl
from jax.experimental.pallas import tpu as pltpu
from jax.sharding import PartitionSpec as P

QUERY_HEADS = 32
KEY_VALUE_HEADS = 2
HEAD_SIZE = 128


neg_fill = -1e30
eps_norm = 1e-06


MESH = pl.DeviceIdType.MESH
NX, NY, NZ, NYL = 4, 4, 8, 2
CHUNKS = 16
CAP = 6
PEERS = NX * NY
PEER_ROWS = NZ * CAP
COLUMN_ROWS = NY * PEER_ROWS
SLOT_ROWS = PEERS * PEER_ROWS
SECOND_LAG = 2
MULTIPLY_LAG = 4


def position():
    g, i = lax.axis_index("grp"), lax.axis_index("exp")
    x, y_hi = lax.div(g, 2), lax.rem(g, 2)
    z, y_lo, core = lax.div(i, 4), lax.rem(lax.div(i, 2), 2), lax.rem(i, 2)
    return x, y_hi * 2 + y_lo, z, core


def device(x, y, z, core):
    return (x * 2 + lax.div(y, 2), (z * 2 + lax.rem(y, 2)) * 2 + core)


def remote(src, dst, send, recv, to):
    return pltpu.make_async_remote_copy(
        src_ref=src, dst_ref=dst, send_sem=send, recv_sem=recv, device_id=to, device_id_type=MESH
    )


def wait_bytes(ref, sem):
    pltpu.make_async_copy(ref, ref, sem).wait()


def plane_expert(rows, z):
    row = lax.broadcasted_iota(jnp.int32, (rows, 1), 0).astype(jnp.float32)
    place = jnp.floor((row + 0.5) * (1.0 / PEER_ROWS))
    within = row - place * PEER_ROWS
    source = jnp.floor((within + 0.5) * (1.0 / CAP))
    slot = within - source * CAP
    px = jnp.floor((place + 0.5) * (1.0 / NY))
    py = place - px * NY
    py_hi = jnp.floor((py + 0.5) * 0.5)
    expert = px * (4 * NZ) + py_hi * (2 * NZ) + (py - py_hi * 2) + (z * 2).astype(jnp.float32)
    lane = lax.broadcasted_iota(jnp.int32, (rows, 128), 1).astype(jnp.float32)
    return lane == expert, source, slot


def dispatch_kernel(
    x_hbm,
    weight_ref,
    sel_hbm,
    gu_ref,
    out_ref,
    sel,
    xall,
    weights,
    wbuf,
    sendb,
    mid,
    recvb,
    wsend,
    wmid,
    wrecv,
    acc,
    outsend,
    z_right,
    z_left,
    z_send,
    weight_right,
    weight_left,
    weight_send,
    x_send,
    x_recv,
    y_send,
    y_recv,
    w_sems,
    gu_sems,
    out_sems,
    load_sems,
):
    x, y, z, core = position()
    up, down = lax.rem(z + 1, NZ), lax.rem(z + NZ - 1, NZ)
    up_dev, down_dev = device(x, y, up, core), device(x, y, down, core)
    sibling = device(x, y, z, 1 - core)
    xs = [lax.rem(x + d, NX) for d in range(NX)]
    ys = [lax.rem(y + d, NY) for d in range(NY)]
    x_dev = [device(xs[d], y, z, core) for d in range(NX)]
    y_dev = [device(x, ys[d], z, core) for d in range(NY)]
    width = x_hbm.shape[1] // CHUNKS
    order = (2, 1, 3)

    barrier = pltpu.get_barrier_semaphore()
    partners = x_dev[1:] + y_dev[1:] + [up_dev, down_dev, sibling]
    for to in partners:
        pl.semaphore_signal(barrier, inc=1, device_id=to, device_id_type=MESH)

    def weight_hop(step, right):
        if right:
            block, to, sem = lax.rem(z + NZ - step, NZ), up_dev, weight_right
        else:
            block, to, sem = lax.rem(z + step, NZ), down_dev, weight_left
        return remote(weights.at[block], weights.at[block], weight_send.at[0], sem.at[step], to)

    def hop(k, step, right):
        if right:
            block, to, sem = lax.rem(z + NZ - step, NZ), up_dev, z_right
        else:
            block, to, sem = lax.rem(z + step, NZ), down_dev, z_left
        return remote(xall.at[k, block], xall.at[k, block], z_send.at[k], sem.at[k, step], to)

    def along_x(src, dst, send, recv):
        for d in order:
            remote(src.at[xs[d]], dst.at[x], send, recv, x_dev[d]).start()

    def along_y(src, dst, send, recv):
        for d in order:
            remote(src.at[:, ys[d]], dst.at[y], send, recv, y_dev[d]).start()

    own_copy = pltpu.make_async_copy(gu_ref, wbuf.at[core], gu_sems.at[0])
    other_copy = remote(gu_ref, wbuf.at[core], gu_sems.at[1], gu_sems.at[2], sibling)
    def load(k):
        cols = pl.ds(pl.multiple_of(k * width, width), width)
        return pltpu.make_async_copy(x_hbm.at[:, cols], xall.at[k, z], load_sems.at[k])

    def load_start(k, carry):
        load(k).start()
        return carry

    lax.fori_loop(0, CHUNKS, load_start, 0)
    sel_load = pltpu.make_async_copy(sel_hbm, sel, load_sems.at[CHUNKS])
    sel_load.start()
    own_copy.start()
    weights[z] = weight_ref[...]

    def zero(r, carry):
        rows = pl.ds(pl.multiple_of(lax.rem(r, NX) * COLUMN_ROWS, COLUMN_ROWS), COLUMN_ROWS)
        acc[lax.div(r, NX), rows, :] = jnp.zeros((COLUMN_ROWS, acc.shape[2]), jnp.float32)
        return carry

    lax.fori_loop(0, 2 * NX, zero, 0)

    pl.semaphore_wait(barrier, len(partners))
    for k in range(2):
        load(k).wait()
        hop(k, 0, True).start()
        hop(k, 0, False).start()
    weight_hop(0, True).start()
    weight_hop(0, False).start()
    other_copy.start()

    def tick(t, carry):
        for step in (4, 3, 2, 1):
            k = t - step

            @pl.when((k >= 0) & (k < CHUNKS))
            def _():
                even = lax.rem(k, 2) == 0
                if step == 4:

                    @pl.when(even)
                    def _():
                        hop(k, 3, True).wait_recv()

                    @pl.when(jnp.logical_not(even))
                    def _():
                        hop(k, 3, False).wait_recv()
                else:
                    hop(k, step - 1, True).wait_recv()
                    if step < 3:
                        hop(k, step, True).start()
                    else:

                        @pl.when(even)
                        def _():
                            hop(k, step, True).start()

                    hop(k, step - 1, False).wait_recv()
                    if step < 3:
                        hop(k, step, False).start()
                    else:

                        @pl.when(jnp.logical_not(even))
                        def _():
                            hop(k, step, False).start()

        @pl.when(t + 2 < CHUNKS)
        def _():
            load(t + 2).wait()
            hop(t + 2, 0, True).start()
            hop(t + 2, 0, False).start()

        @pl.when((t >= 1) & (t <= 4))
        def _():
            weight_hop(t - 1, True).wait_recv()

            @pl.when(t < 4)
            def _():
                weight_hop(t - 1, False).wait_recv()
                weight_hop(t, True).start()

            @pl.when(t < 3)
            def _():
                weight_hop(t, False).start()

        k_sel = t - 4

        @pl.when((k_sel >= 0) & (k_sel < CHUNKS))
        def _():
            @pl.when(k_sel == 0)
            def _():
                sel_load.wait()

            picked = jnp.dot(
                sel[...], xall[k_sel].reshape(-1, width), preferred_element_type=jnp.float32
            )
            sendb[k_sel] = picked.astype(jnp.bfloat16).reshape(NX, NY, PEER_ROWS, width)
            along_x(sendb.at[k_sel], mid.at[k_sel], x_send.at[k_sel], x_recv.at[k_sel])
            mid[k_sel, x] = sendb[k_sel, x]

        @pl.when(t == 6)
        def _():
            chosen, _, _ = plane_expert(SLOT_ROWS, z)
            spread = jnp.dot(
                sel[...], weights[...].reshape(-1, weights.shape[2]), preferred_element_type=jnp.float32
            )
            column = jnp.sum(jnp.where(chosen, spread, 0.0), axis=1, keepdims=True)
            wsend[...] = (
                jnp.broadcast_to(column, (SLOT_ROWS, 128)).astype(jnp.bfloat16).reshape(wsend.shape)
            )
            along_x(wsend, wmid, w_sems.at[0], w_sems.at[1])
            wmid[x] = wsend[x]

        @pl.when(t == 9)
        def _():
            wait_bytes(wmid.at[pl.ds(0, NX - 1)], w_sems.at[1])
            along_y(wmid, wrecv, w_sems.at[2], w_sems.at[3])
            wrecv[y] = wmid[:, y]

        k_mid = t - 4 - SECOND_LAG

        @pl.when((k_mid >= 0) & (k_mid < CHUNKS))
        def _():
            wait_bytes(mid.at[k_mid, pl.ds(0, NX - 1)], x_recv.at[k_mid])
            along_y(mid.at[k_mid], recvb.at[k_mid], y_send.at[k_mid], y_recv.at[k_mid])
            recvb[k_mid, y] = mid[k_mid, :, y]

        k_mul = t - 4 - MULTIPLY_LAG

        @pl.when(k_mul >= 0)
        def _():
            @pl.when(k_mul == 0)
            def _():
                own_copy.wait()
                other_copy.wait_recv()

            wait_bytes(recvb.at[k_mul, pl.ds(0, NY - 1)], y_recv.at[k_mul])
            cols = pl.ds(pl.multiple_of(k_mul * width, width), width)

            def multiply(r, c):
                h = lax.div(r, 3)
                inner = pl.ds(pl.multiple_of(lax.rem(r, 3) * 256, 256), 256)
                acc[h, :, inner] += jnp.dot(
                    recvb[k_mul].reshape(SLOT_ROWS, width),
                    wbuf[h, cols, inner],
                    preferred_element_type=jnp.float32,
                )
                return c

            lax.fori_loop(0, 6, multiply, 0)

        return carry

    lax.fori_loop(0, CHUNKS + 4 + MULTIPLY_LAG, tick, 0)

    wait_bytes(wrecv.at[pl.ds(0, NY - 1)], w_sems.at[3])
    half = acc.shape[2] // 2

    def finish(h, part):
        rows = pl.ds(pl.multiple_of(part * COLUMN_ROWS, COLUMN_ROWS), COLUMN_ROWS)
        gate, lift = acc[h, rows, :half], acc[h, rows, half:]
        weight = wrecv[part].reshape(COLUMN_ROWS, 128)[:, :1].astype(jnp.float32)
        return rows, (weight * (gate / (1.0 + jnp.exp(-gate))) * lift).astype(jnp.bfloat16)

    def finish_other(part, c):
        rows, values = finish(1 - core, part)
        outsend[rows, :] = values
        return c

    def finish_own(part, c):
        rows, values = finish(core, part)
        out_ref[core, rows, :] = values
        return c

    lax.fori_loop(0, NY, finish_other, 0)
    out_copy = remote(outsend, out_ref.at[core], out_sems.at[0], out_sems.at[1], sibling)
    out_copy.start()
    lax.fori_loop(0, NY, finish_own, 0)

    def drain(k, c):
        wait_bytes(xall.at[k, pl.ds(0, NZ - 1)], z_send.at[k])
        wait_bytes(sendb.at[k, pl.ds(0, NX - 1)], x_send.at[k])
        wait_bytes(mid.at[k, pl.ds(0, NX - 1)], y_send.at[k])
        return c

    lax.fori_loop(0, CHUNKS, drain, 0)
    wait_bytes(weights.at[pl.ds(0, NZ - 1)], weight_send.at[0])
    wait_bytes(wsend.at[pl.ds(0, NX - 1)], w_sems.at[0])
    wait_bytes(wmid.at[pl.ds(0, NX - 1)], w_sems.at[2])
    other_copy.wait_send()
    out_copy.wait()


def dispatch(normed, weight, sel, gate_up):
    tokens, model = normed.shape
    width = model // CHUNKS
    inner = gate_up.shape[1]
    vmem, hbm = pl.BlockSpec(memory_space=pltpu.VMEM), pl.BlockSpec(memory_space=pl.ANY)
    dma = pltpu.SemaphoreType.DMA
    rows = (NX, NY, PEER_ROWS)
    return pl.pallas_call(
        dispatch_kernel,
        out_shape=jax.ShapeDtypeStruct((2, SLOT_ROWS, inner // 2), jnp.bfloat16),
        in_specs=[hbm, vmem, hbm, hbm],
        out_specs=vmem,
        scratch_shapes=[
            pltpu.VMEM(sel.shape, jnp.bfloat16),
            pltpu.VMEM((CHUNKS, NZ, tokens, width), jnp.bfloat16),
            pltpu.VMEM((NZ, tokens, 128), jnp.bfloat16),
            pltpu.VMEM((2, model, inner), jnp.bfloat16),
            pltpu.VMEM((CHUNKS, *rows, width), jnp.bfloat16),
            pltpu.VMEM((CHUNKS, *rows, width), jnp.bfloat16),
            pltpu.VMEM((CHUNKS, *rows, width), jnp.bfloat16),
            pltpu.VMEM((*rows, 128), jnp.bfloat16),
            pltpu.VMEM((*rows, 128), jnp.bfloat16),
            pltpu.VMEM((*rows, 128), jnp.bfloat16),
            pltpu.VMEM((2, SLOT_ROWS, inner), jnp.float32),
            pltpu.VMEM((SLOT_ROWS, inner // 2), jnp.bfloat16),
            dma((CHUNKS, 4)),
            dma((CHUNKS, 4)),
            dma((CHUNKS,)),
            dma((4,)),
            dma((4,)),
            dma((1,)),
            dma((CHUNKS,)),
            dma((CHUNKS,)),
            dma((CHUNKS,)),
            dma((CHUNKS,)),
            dma((4,)),
            dma((3,)),
            dma((2,)),
            dma((CHUNKS + 1,)),
        ],
        compiler_params=pltpu.CompilerParams(
            collective_id=1, has_side_effects=True, vmem_limit_bytes=62 * 1024 * 1024
        ),
        cost_estimate=pl.CostEstimate(
            flops=2 * SLOT_ROWS * model * (2 * inner + NZ * tokens),
            bytes_accessed=model * inner * 2,
            transcendentals=0,
        ),
        name="dispatch",
    )(normed, weight, sel, gate_up)


def attend_kernel(
    prompt_rows,
    q_hbm,
    kv_ref,
    prompt_ref,
    lengths_ref,
    w_hbm,
    hidden_hbm,
    gain_ref,
    router_hbm,
    routes_ref,
    resid_ref,
    normed_ref,
    weight_ref,
    sel_ref,
    q_ref,
    hidden_ref,
    router_ref,
    bias_ref,
    ranks,
    wc,
    pbuf,
    kvbuf,
    kcat,
    vcat,
    ctx,
    send_out,
    recv_out,
    load_sems,
    rank_sems,
    prompt_sems,
    kv_sems,
    z_recv,
    z_send,
    near_recv,
    spread_send,
    x_direct,
    x_relay,
    y_direct,
    y_relay,
    ctx_send,
    ctx_recv,
    out_send,
    out_recv,
):
    x, y, z, core = position()
    y_hi, y_lo = lax.div(y, 2), lax.rem(y, 2)
    z_pair, z_side = lax.div(z, 2), lax.rem(z, 2)
    xs = [lax.rem(x + d, NX) for d in range(NX)]
    ys = [lax.rem(y + d, NY) for d in range(NY)]
    x_dev = [device(xs[d], y, z, core) for d in range(NX)]
    y_dev = [device(x, ys[d], z, core) for d in range(NY)]
    z_dev = [device(x, y, lax.rem(z + d, NZ), core) for d in range(NZ)]
    sibling = device(x, y, z, 1 - core)
    twin = device(x, y, z_pair * 2 + 1 - z_side, core)
    cross = device(x, y, z_pair * 2 + 1 - z_side, 1 - core)
    pair_dev = device(x, y_hi * 2 + 1 - y_lo, z, core)

    barrier = pltpu.get_barrier_semaphore()
    partners = x_dev[1:] + y_dev[1:] + z_dev[1:] + [sibling, cross]
    for to in partners:
        pl.semaphore_signal(barrier, inc=1, device_id=to, device_id_type=MESH)

    steps = NZ // 2
    chunks = [lax.rem(z_pair + d, steps) for d in (0, 1, 3, 2)]

    def own_shard(half):
        return w_hbm.at[pl.ds(half * 256, 256)]

    def near(j, half, d, src):
        part = wc.at[j, y_lo, x, y_hi, half]
        to = (y_dev, x_dev)[half][d]
        remote(src, part, spread_send.at[j, 1], near_recv.at[j, half, d - 1], to).start()

    def xpart(j, d):
        return wc.at[j, :, xs[d], :, 0]

    def ypart(j, d):
        return wc.at[j, lax.rem(ys[d], 2), :, lax.div(ys[d], 2), 1]

    def xhalf(j, d, which):
        return wc.at[j, :, xs[d], which, 0]

    def yhalf(j, d, which):
        return wc.at[j, lax.rem(ys[d], 2), pl.ds(2 * which, 2), lax.div(ys[d], 2), 1]

    def begin(j):
        for d in (1, 3, 2):
            for half in range(2):
                near(j, half, d, wc.at[j, y_lo, x, y_hi, half])

    def spread(j):
        for half in range(2):
            for d in (1, 3, 2):
                if half == 0:
                    part = wc.at[j, lax.rem(ys[4 - d], 2), x, lax.div(ys[4 - d], 2), 0]
                else:
                    part = wc.at[j, y_lo, xs[4 - d], y_hi, 1]
                wait_bytes(part, near_recv.at[j, half, d - 1])
            parts, devs, sem = ((xpart, x_dev, x_direct), (ypart, y_dev, y_direct))[half]
            part = parts(j, 0)
            remote(part, part, spread_send.at[j, 0], sem.at[j, 0], devs[1]).start()
            remote(part, part, spread_send.at[j, 0], sem.at[j, 1], devs[3]).start()

    def relay(j):
        for parts, halves, devs, sem, next_sem in (
            (xpart, xhalf, x_dev, x_direct, x_relay),
            (ypart, yhalf, y_dev, y_direct, y_relay),
        ):
            wait_bytes(parts(j, 3), sem.at[j, 0])
            part = halves(j, 3, 0)
            remote(part, part, spread_send.at[j, 0], next_sem.at[j, 0], devs[1]).start()
            wait_bytes(parts(j, 1), sem.at[j, 1])
            part = halves(j, 1, 1)
            remote(part, part, spread_send.at[j, 0], next_sem.at[j, 1], devs[3]).start()

    def settle(j):
        for halves, next_sem in ((xhalf, x_relay), (yhalf, y_relay)):
            for which in range(2):
                wait_bytes(halves(j, 2, which), next_sem.at[j, which])

    tokens = kv_ref.shape[0]
    own_weight = [
        pltpu.make_async_copy(own_shard(half), wc.at[z_pair, y_lo, x, y_hi, half], load_sems.at[half])
        for half in range(2)
    ]
    for copy in own_weight:
        copy.start()
    spare = jnp.zeros((pbuf.shape[3] - prompt_rows, pbuf.shape[4]), jnp.float32)
    pbuf[core, y_lo, z] = jnp.concatenate([prompt_ref[...].astype(jnp.float32), spare], axis=0).astype(
        jnp.bfloat16
    )
    loads = [
        pltpu.make_async_copy(src, dst, load_sems.at[2 + i])
        for i, (src, dst) in enumerate(((q_hbm, q_ref), (hidden_hbm, hidden_ref), (router_hbm, router_ref)))
    ]
    for copy in loads:
        copy.start()
    kvbuf[core] = kv_ref[...]
    lane = lax.broadcasted_iota(jnp.int32, (tokens, 128), 1)
    row = lax.broadcasted_iota(jnp.int32, (tokens, 128), 0)
    named = routes_ref[0:1, :] == row
    for k in range(1, routes_ref.shape[0]):
        named = named | (routes_ref[k : k + 1, :] == row)
    earlier = jnp.where(row <= lane, 1.0, 0.0).astype(jnp.bfloat16)
    counted = jnp.dot(
        jnp.where(named, 1.0, 0.0).astype(jnp.bfloat16), earlier, preferred_element_type=jnp.float32
    )
    ranks[z] = jnp.where(named, counted, 0.0).astype(jnp.bfloat16)
    keys = bias_ref.shape[1]
    held = keys - 2 * tokens
    length = lengths_ref[0, z * 2 + y_lo]
    place = lax.broadcasted_iota(jnp.int32, (tokens, held), 1)
    bias_ref[:, :held] = jnp.where((place & 15) < prompt_rows, 0.0, neg_fill)
    place = lax.broadcasted_iota(jnp.int32, (tokens, 2 * tokens), 1)
    moment = lax.broadcasted_iota(jnp.int32, (tokens, 2 * tokens), 0) + core * tokens
    bias_ref[:, held:] = jnp.where((place <= moment) & (place < length), 0.0, neg_fill)

    pl.semaphore_wait(barrier, len(partners))
    for d in (1, 3, 2):
        for half in range(2):
            near(z_pair, half, d, own_shard(half))
    for d in (4, 3, 5, 2, 6, 1, 7):
        part = pbuf.at[core, y_lo, z]
        remote(part, part, prompt_sems.at[0], prompt_sems.at[5], z_dev[d]).start()
    for d in (1, 3, 2):
        for half in range(2):
            part = wc.at[z_pair, y_lo, x, y_hi, half]
            remote(own_shard(half), part, z_send.at[0], z_recv.at[half, d - 1], z_dev[2 * d]).start()
    kv_copy = remote(kv_ref, kvbuf.at[core], kv_sems.at[0], kv_sems.at[1], sibling)
    kv_copy.start()

    wait_bytes(pbuf.at[core, y_lo, pl.ds(0, NZ - 1)], prompt_sems.at[5])
    part = pbuf.at[core, y_lo]
    prompt_pair = remote(part, part, prompt_sems.at[1], prompt_sems.at[2], pair_dev)
    prompt_pair.start()
    for copy in own_weight:
        copy.wait()
    spread(chunks[0])

    for d in (4, 3, 5, 2, 6, 1, 7):
        remote(ranks.at[z], ranks.at[z], rank_sems.at[0], rank_sems.at[1], z_dev[d]).start()

    wait_bytes(pbuf.at[core, 1 - y_lo], prompt_sems.at[2])
    prompt_sib = remote(pbuf.at[core], pbuf.at[core], prompt_sems.at[3], prompt_sems.at[4], sibling)
    prompt_sib.start()
    for d, j in ((1, chunks[2]), (3, chunks[1]), (2, chunks[3])):
        for half in range(2):
            wait_bytes(wc.at[j, y_lo, x, y_hi, half], z_recv.at[half, d - 1])
        begin(j)
    wait_bytes(kvbuf.at[1 - core], kv_sems.at[1])
    wait_bytes(pbuf.at[1 - core], prompt_sems.at[4])
    prompt_keys = pbuf[...].reshape(-1, pbuf.shape[-1])
    own_rows = kvbuf[...].reshape(2 * tokens, kvbuf.shape[-1])
    for g in range(KEY_VALUE_HEADS):
        low, high = g * HEAD_SIZE, (KEY_VALUE_HEADS + g) * HEAD_SIZE
        kcat[g, :held, :] = prompt_keys[:, low : low + HEAD_SIZE]
        kcat[g, held:, :] = own_rows[:, low : low + HEAD_SIZE]
        vcat[g, :held, :] = prompt_keys[:, high : high + HEAD_SIZE]
        vcat[g, held:, :] = own_rows[:, high : high + HEAD_SIZE]
    loads[0].wait()

    pairs = QUERY_HEADS // 2
    sections = ctx.shape[2]

    def attend(section, i, carry):
        g = section * KEY_VALUE_HEADS // sections
        j = section * (pairs // sections) + i
        query = jnp.concatenate(
            [
                q_ref[:, pl.ds(pl.multiple_of((j * 2 + n) * HEAD_SIZE, HEAD_SIZE), HEAD_SIZE)]
                for n in range(2)
            ],
            axis=0,
        )
        scores = lax.dot_general(
            query, kcat[g], (((1,), (1,)), ((), ())), preferred_element_type=jnp.float32
        )
        scores = scores * (HEAD_SIZE**-0.5) + jnp.concatenate([bias_ref[...], bias_ref[...]], axis=0)
        raised = jnp.exp(scores - jnp.max(scores, axis=1, keepdims=True))
        denom = jnp.sum(raised, axis=1, keepdims=True)
        mixed = jnp.dot(raised.astype(jnp.bfloat16), vcat[g], preferred_element_type=jnp.float32)
        mixed = (mixed / denom).astype(jnp.bfloat16)
        for n in range(2):
            cols = pl.ds(pl.multiple_of((i * 2 + n) * HEAD_SIZE, HEAD_SIZE), HEAD_SIZE)
            ctx[z_side, core, section, :, cols] = mixed[n * tokens : (n + 1) * tokens]
        return carry

    def ctx_move(section, side, to, which):
        part = ctx.at[side, core, section]
        return remote(part, part, ctx_send.at[section, which], ctx_recv.at[section, which], to)

    for section in range(sections):
        lax.fori_loop(0, pairs // sections, functools.partial(attend, section), 0)
        ctx_move(section, z_side, twin, 0).start()
        ctx_move(section, z_side, sibling, 1).start()
        if section == 0:
            spread(chunks[2])
            relay(chunks[0])
            spread(chunks[1])
    relay(chunks[2])
    spread(chunks[3])
    relay(chunks[1])

    wait_bytes(ranks.at[pl.ds(0, NZ - 1)], rank_sems.at[1])
    chosen, source, slot = plane_expert(SLOT_ROWS, z)
    picker = jnp.where(chosen, 1.0, 0.0).astype(jnp.bfloat16)
    for b in range(NZ):
        found = jnp.dot(picker, ranks[b], preferred_element_type=jnp.float32)
        hit = (found == slot + 1.0) & (source == float(b))
        sel_ref[:, b * tokens : (b + 1) * tokens] = jnp.where(hit, 1.0, 0.0).astype(jnp.bfloat16)

    relay(chunks[3])
    for section in range(sections):
        wait_bytes(ctx.at[1 - z_side, core, section], ctx_recv.at[section, 0])
        ctx_move(section, 1 - z_side, sibling, 2).start()
    for section in range(sections):
        wait_bytes(ctx.at[z_side, 1 - core, section], ctx_recv.at[section, 1])
        wait_bytes(ctx.at[1 - z_side, 1 - core, section], ctx_recv.at[section, 2])

    def out_move(j, side, who, to, which):
        return remote(
            send_out.at[j, side, who],
            recv_out.at[z_side, core, j],
            out_send.at[j, which],
            out_recv.at[j, which],
            to,
        )

    def out_moves(j):
        return (
            out_move(j, 1 - z_side, core, twin, 0),
            out_move(j, 1 - z_side, 1 - core, cross, 1),
            out_move(j, z_side, 1 - core, sibling, 2),
        )

    deep = 4096 // NX

    def project(j):
        settle(j)

        def part(i, total):
            cols = pl.ds(pl.multiple_of(lax.rem(i, 2) * deep, deep), deep)
            left = ctx[:, :, lax.div(i, 2), :, cols].reshape(4 * tokens, deep)
            right = jnp.concatenate(
                [wc[j, 0, i].reshape(deep, 128), wc[j, 1, i].reshape(deep, 128)], axis=1
            )
            return total + jnp.dot(left, right, preferred_element_type=jnp.float32)

        total = lax.fori_loop(0, NX, part, jnp.zeros((4 * tokens, 256), jnp.float32))
        send_out[j] = total.astype(jnp.bfloat16).reshape(2, 2, tokens, 256)
        for move in out_moves(j):
            move.start()
        recv_out[z_side, core, j] = send_out[j, z_side, core]

    def chunk_at(i):
        d = jnp.where(i == 1, 3, jnp.where(i == 2, 1, jnp.where(i == 3, 2, 0)))
        return lax.rem(z_pair + d, steps)

    def project_at(i, carry):
        project(chunk_at(i))
        return carry

    def add_up(i, square):
        j = chunk_at(i)
        wait_bytes(recv_out.at[1 - z_side, core, j], out_recv.at[j, 0])
        wait_bytes(recv_out.at[1 - z_side, 1 - core, j], out_recv.at[j, 1])
        wait_bytes(recv_out.at[z_side, 1 - core, j], out_recv.at[j, 2])
        for side in range(2):
            for lo in range(2):
                for who in range(2):
                    cols = pl.ds(pl.multiple_of((((j * 2 + side) * 2 + lo) * 2 + who) * 128, 128), 128)
                    part = recv_out[side, who, j, :, lo * 128 : (lo + 1) * 128].astype(jnp.float32)
                    rounded = (hidden_ref[:, cols].astype(jnp.float32) + part).astype(jnp.bfloat16)
                    resid_ref[:, cols] = rounded
                    wide = rounded.astype(jnp.float32)
                    square = square + wide * wide
        return square

    lax.fori_loop(0, steps, project_at, 0)
    loads[1].wait()
    loads[2].wait()
    square = lax.fori_loop(0, steps, add_up, jnp.zeros((tokens, 128), jnp.float32))
    model = hidden_ref.shape[1]
    scale = lax.rsqrt(jnp.sum(square, axis=1, keepdims=True) * (1.0 / model) + eps_norm)

    def normalise(i, logits):
        cols = pl.ds(pl.multiple_of(i * 512, 512), 512)
        part = (resid_ref[:, cols].astype(jnp.float32) * scale * gain_ref[:, cols]).astype(jnp.bfloat16)
        normed_ref[:, cols] = part
        return logits + jnp.dot(part, router_ref[cols, :], preferred_element_type=jnp.float32)

    logits = lax.fori_loop(0, model // 512, normalise, jnp.zeros((tokens, 128), jnp.float32))
    named = ranks[z].astype(jnp.float32).T > 0.0
    masked = jnp.where(named, logits, neg_fill)
    raised = jnp.where(named, jnp.exp(masked - jnp.max(masked, axis=1, keepdims=True)), 0.0)
    weight_ref[...] = (raised / jnp.sum(raised, axis=1, keepdims=True)).astype(jnp.bfloat16)

    kv_copy.wait_send()
    wait_bytes(ranks.at[pl.ds(0, NZ - 1)], rank_sems.at[0])
    wait_bytes(pbuf.at[0, 0, pl.ds(0, NZ - 1)], prompt_sems.at[0])
    prompt_pair.wait_send()
    prompt_sib.wait_send()
    wait_bytes(wc.at[0, 0, pl.ds(0, 3), :, 0], z_send.at[0])
    for section in range(sections):
        for which in range(3):
            wait_bytes(ctx.at[z_side, core, section], ctx_send.at[section, which])

    def drain(j, carry):
        wait_bytes(wc.at[j, :, pl.ds(0, 3)], spread_send.at[j, 0])
        wait_bytes(wc.at[j, 0, pl.ds(0, 3), :, 0], spread_send.at[j, 1])
        for move in out_moves(j):
            move.wait_send()
        return carry

    lax.fori_loop(0, steps, drain, 0)


def attend_all(queries, key_value, prompt, lengths, out_weight, hidden, gain, router, routes):
    tokens, model = queries.shape
    vmem, hbm = pl.BlockSpec(memory_space=pltpu.VMEM), pl.BlockSpec(memory_space=pl.ANY)
    smem = pl.BlockSpec(memory_space=pltpu.SMEM)
    dma = pltpu.SemaphoreType.DMA
    kv_width = key_value.shape[1]
    prompt_rows = prompt.shape[0]
    held_rows = -(-prompt_rows // 16) * 16
    keys = 2 * NYL * NZ * held_rows + 2 * tokens
    experts = router.shape[1]
    return pl.pallas_call(
        functools.partial(attend_kernel, prompt_rows),
        out_shape=(
            jax.ShapeDtypeStruct((tokens, model), jnp.bfloat16),
            jax.ShapeDtypeStruct((tokens, model), jnp.bfloat16),
            jax.ShapeDtypeStruct((tokens, experts), jnp.bfloat16),
            jax.ShapeDtypeStruct((SLOT_ROWS, NZ * tokens), jnp.bfloat16),
        ),
        in_specs=[hbm, vmem, vmem, smem, hbm, hbm, vmem, hbm, vmem],
        out_specs=[vmem] * 4,
        scratch_shapes=[
            pltpu.VMEM((tokens, model), jnp.bfloat16),
            pltpu.VMEM((tokens, model), jnp.bfloat16),
            pltpu.VMEM((model, experts), jnp.bfloat16),
            pltpu.VMEM((tokens, keys), jnp.float32),
            pltpu.VMEM((NZ, tokens, experts), jnp.bfloat16),
            pltpu.VMEM((NZ // 2, 2, NX, 2, 2, 256, 128), jnp.bfloat16),
            pltpu.VMEM((2, 2, NZ, held_rows, kv_width), jnp.bfloat16),
            pltpu.VMEM((2, tokens, kv_width), jnp.bfloat16),
            pltpu.VMEM((KEY_VALUE_HEADS, keys, HEAD_SIZE), jnp.bfloat16),
            pltpu.VMEM((KEY_VALUE_HEADS, keys, HEAD_SIZE), jnp.bfloat16),
            pltpu.VMEM((2, 2, 2, tokens, model // 2), jnp.bfloat16),
            pltpu.VMEM((NZ // 2, 2, 2, tokens, 256), jnp.bfloat16),
            pltpu.VMEM((2, 2, NZ // 2, tokens, 256), jnp.bfloat16),
            dma((5,)),
            dma((2,)),
            dma((6,)),
            dma((2,)),
            dma((2, 3)),
            dma((1,)),
            dma((NZ // 2, 2, 3)),
            dma((NZ // 2, 2)),
            dma((NZ // 2, 2)),
            dma((NZ // 2, 2)),
            dma((NZ // 2, 2)),
            dma((NZ // 2, 2)),
            dma((2, 3)),
            dma((2, 3)),
            dma((NZ // 2, 3)),
            dma((NZ // 2, 3)),
        ],
        compiler_params=pltpu.CompilerParams(
            collective_id=2, has_side_effects=True, vmem_limit_bytes=62 * 1024 * 1024
        ),
        cost_estimate=pl.CostEstimate(
            flops=2 * tokens * model * (model + 2 * keys), bytes_accessed=8 * tokens * model, transcendentals=0
        ),
        name="attend",
    )(queries, key_value, prompt, lengths, out_weight, hidden, gain, router, routes)


def local(
    hidden,
    queries,
    response_key_value,
    prompt_kv,
    lengths,
    out_weight,
    norm_gain,
    router,
    gate_up,
    routes,
):
    resid_out, normed, weight, sel = attend_all(
        queries[0],
        response_key_value[0],
        prompt_kv[0],
        lengths,
        out_weight,
        hidden[0],
        norm_gain[None, :],
        router,
        routes[0].T,
    )
    slots = dispatch(normed, weight, sel, gate_up[0])
    expert_act = (
        slots.reshape(2, 2, 2, NX, NZ, CAP, -1)
        .transpose(3, 1, 4, 2, 0, 5, 6)
        .reshape(1, 2 * NX * NZ * NY, CAP, -1)
    )
    return (resid_out[None], expert_act)


def solution(mesh):
    placed = (
        P("grp", "exp", None),
        P("grp", "exp", None),
        P("grp", "exp", None),
        P("grp", "exp", None),
        P("grp", None),
        P("grp", "exp"),
        P(),
        P(),
        P(("grp", "exp"), None, None),
        P("grp", "exp", None),
    )
    return jax.shard_map(
        local,
        mesh=mesh,
        in_specs=placed,
        out_specs=(P("grp", "exp", None), P(("grp", "exp"), None, None, None)),
        check_vma=False,
    )
```

```python
import functools

import jax
import jax.numpy as jnp
from jax import lax
from jax.experimental import pallas as pl
from jax.experimental.pallas import tpu as pltpu
from jax.sharding import PartitionSpec as P

QUERY_HEADS = 32
KEY_VALUE_HEADS = 2
HEAD_SIZE = 128


neg_fill = -1e30
eps_norm = 1e-06


MESH = pl.DeviceIdType.MESH
NX, NY, NZ, NYL = 4, 4, 8, 2
CHUNKS = 16
CAP = 6
PEERS = NX * NY
PEER_ROWS = NZ * CAP
COLUMN_ROWS = NY * PEER_ROWS
SLOT_ROWS = PEERS * PEER_ROWS
SECOND_LAG = 2
MULTIPLY_LAG = 4


def position():
    g, i = lax.axis_index("grp"), lax.axis_index("exp")
    x, y_hi = lax.div(g, 2), lax.rem(g, 2)
    z, y_lo, core = lax.div(i, 4), lax.rem(lax.div(i, 2), 2), lax.rem(i, 2)
    return x, y_hi * 2 + y_lo, z, core


def device(x, y, z, core):
    return (x * 2 + lax.div(y, 2), (z * 2 + lax.rem(y, 2)) * 2 + core)


def remote(src, dst, send, recv, to):
    return pltpu.make_async_remote_copy(
        src_ref=src, dst_ref=dst, send_sem=send, recv_sem=recv, device_id=to, device_id_type=MESH
    )


def wait_bytes(ref, sem):
    pltpu.make_async_copy(ref, ref, sem).wait()


def plane_expert(rows, z):
    row = lax.broadcasted_iota(jnp.int32, (rows, 1), 0).astype(jnp.float32)
    place = jnp.floor((row + 0.5) * (1.0 / PEER_ROWS))
    within = row - place * PEER_ROWS
    source = jnp.floor((within + 0.5) * (1.0 / CAP))
    slot = within - source * CAP
    px = jnp.floor((place + 0.5) * (1.0 / NY))
    py = place - px * NY
    py_hi = jnp.floor((py + 0.5) * 0.5)
    expert = px * (4 * NZ) + py_hi * (2 * NZ) + (py - py_hi * 2) + (z * 2).astype(jnp.float32)
    lane = lax.broadcasted_iota(jnp.int32, (rows, 128), 1).astype(jnp.float32)
    return lane == expert, source, slot


def dispatch_kernel(
    x_hbm,
    weight_ref,
    sel_hbm,
    gu_ref,
    out_ref,
    sel,
    xall,
    weights,
    wbuf,
    sendb,
    mid,
    recvb,
    wsend,
    wmid,
    wrecv,
    acc,
    outsend,
    z_right,
    z_left,
    z_send,
    weight_right,
    weight_left,
    weight_send,
    x_send,
    x_recv,
    y_send,
    y_recv,
    w_sems,
    gu_sems,
    out_sems,
    load_sems,
):
    x, y, z, core = position()
    up, down = lax.rem(z + 1, NZ), lax.rem(z + NZ - 1, NZ)
    up_dev, down_dev = device(x, y, up, core), device(x, y, down, core)
    sibling = device(x, y, z, 1 - core)
    xs = [lax.rem(x + d, NX) for d in range(NX)]
    ys = [lax.rem(y + d, NY) for d in range(NY)]
    x_dev = [device(xs[d], y, z, core) for d in range(NX)]
    y_dev = [device(x, ys[d], z, core) for d in range(NY)]
    width = x_hbm.shape[1] // CHUNKS
    order = (2, 1, 3)

    barrier = pltpu.get_barrier_semaphore()
    partners = x_dev[1:] + y_dev[1:] + [up_dev, down_dev, sibling]
    for to in partners:
        pl.semaphore_signal(barrier, inc=1, device_id=to, device_id_type=MESH)

    def weight_hop(step, right):
        if right:
            block, to, sem = lax.rem(z + NZ - step, NZ), up_dev, weight_right
        else:
            block, to, sem = lax.rem(z + step, NZ), down_dev, weight_left
        return remote(weights.at[block], weights.at[block], weight_send.at[0], sem.at[step], to)

    def hop(k, step, right):
        if right:
            block, to, sem = lax.rem(z + NZ - step, NZ), up_dev, z_right
        else:
            block, to, sem = lax.rem(z + step, NZ), down_dev, z_left
        return remote(xall.at[k, block], xall.at[k, block], z_send.at[k], sem.at[k, step], to)

    def along_x(src, dst, send, recv):
        for d in order:
            remote(src.at[xs[d]], dst.at[x], send, recv, x_dev[d]).start()

    def along_y(src, dst, send, recv):
        for d in order:
            remote(src.at[:, ys[d]], dst.at[y], send, recv, y_dev[d]).start()

    own_copy = pltpu.make_async_copy(gu_ref, wbuf.at[core], gu_sems.at[0])
    other_copy = remote(gu_ref, wbuf.at[core], gu_sems.at[1], gu_sems.at[2], sibling)
    def load(k):
        cols = pl.ds(pl.multiple_of(k * width, width), width)
        return pltpu.make_async_copy(x_hbm.at[:, cols], xall.at[k, z], load_sems.at[k])

    def load_start(k, carry):
        load(k).start()
        return carry

    lax.fori_loop(0, CHUNKS, load_start, 0)
    sel_load = pltpu.make_async_copy(sel_hbm, sel, load_sems.at[CHUNKS])
    sel_load.start()
    own_copy.start()
    weights[z] = weight_ref[...]

    def zero(r, carry):
        rows = pl.ds(pl.multiple_of(lax.rem(r, NX) * COLUMN_ROWS, COLUMN_ROWS), COLUMN_ROWS)
        acc[lax.div(r, NX), rows, :] = jnp.zeros((COLUMN_ROWS, acc.shape[2]), jnp.float32)
        return carry

    lax.fori_loop(0, 2 * NX, zero, 0)

    pl.semaphore_wait(barrier, len(partners))
    for k in range(2):
        load(k).wait()
        hop(k, 0, True).start()
        hop(k, 0, False).start()
    weight_hop(0, True).start()
    weight_hop(0, False).start()
    other_copy.start()

    def tick(t, carry):
        for step in (4, 3, 2, 1):
            k = t - step

            @pl.when((k >= 0) & (k < CHUNKS))
            def _():
                even = lax.rem(k, 2) == 0
                if step == 4:

                    @pl.when(even)
                    def _():
                        hop(k, 3, True).wait_recv()

                    @pl.when(jnp.logical_not(even))
                    def _():
                        hop(k, 3, False).wait_recv()
                else:
                    hop(k, step - 1, True).wait_recv()
                    if step < 3:
                        hop(k, step, True).start()
                    else:

                        @pl.when(even)
                        def _():
                            hop(k, step, True).start()

                    hop(k, step - 1, False).wait_recv()
                    if step < 3:
                        hop(k, step, False).start()
                    else:

                        @pl.when(jnp.logical_not(even))
                        def _():
                            hop(k, step, False).start()

        @pl.when(t + 2 < CHUNKS)
        def _():
            load(t + 2).wait()
            hop(t + 2, 0, True).start()
            hop(t + 2, 0, False).start()

        @pl.when((t >= 1) & (t <= 4))
        def _():
            weight_hop(t - 1, True).wait_recv()

            @pl.when(t < 4)
            def _():
                weight_hop(t - 1, False).wait_recv()
                weight_hop(t, True).start()

            @pl.when(t < 3)
            def _():
                weight_hop(t, False).start()

        k_sel = t - 4

        @pl.when((k_sel >= 0) & (k_sel < CHUNKS))
        def _():
            @pl.when(k_sel == 0)
            def _():
                sel_load.wait()

            picked = jnp.dot(
                sel[...], xall[k_sel].reshape(-1, width), preferred_element_type=jnp.float32
            )
            sendb[k_sel] = picked.astype(jnp.bfloat16).reshape(NX, NY, PEER_ROWS, width)
            along_x(sendb.at[k_sel], mid.at[k_sel], x_send.at[k_sel], x_recv.at[k_sel])
            mid[k_sel, x] = sendb[k_sel, x]

        @pl.when(t == 6)
        def _():
            chosen, _, _ = plane_expert(SLOT_ROWS, z)
            spread = jnp.dot(
                sel[...], weights[...].reshape(-1, weights.shape[2]), preferred_element_type=jnp.float32
            )
            column = jnp.sum(jnp.where(chosen, spread, 0.0), axis=1, keepdims=True)
            wsend[...] = (
                jnp.broadcast_to(column, (SLOT_ROWS, 128)).astype(jnp.bfloat16).reshape(wsend.shape)
            )
            along_x(wsend, wmid, w_sems.at[0], w_sems.at[1])
            wmid[x] = wsend[x]

        @pl.when(t == 9)
        def _():
            wait_bytes(wmid.at[pl.ds(0, NX - 1)], w_sems.at[1])
            along_y(wmid, wrecv, w_sems.at[2], w_sems.at[3])
            wrecv[y] = wmid[:, y]

        k_mid = t - 4 - SECOND_LAG

        @pl.when((k_mid >= 0) & (k_mid < CHUNKS))
        def _():
            wait_bytes(mid.at[k_mid, pl.ds(0, NX - 1)], x_recv.at[k_mid])
            along_y(mid.at[k_mid], recvb.at[k_mid], y_send.at[k_mid], y_recv.at[k_mid])
            recvb[k_mid, y] = mid[k_mid, :, y]

        k_mul = t - 4 - MULTIPLY_LAG

        @pl.when(k_mul >= 0)
        def _():
            @pl.when(k_mul == 0)
            def _():
                own_copy.wait()
                other_copy.wait_recv()

            wait_bytes(recvb.at[k_mul, pl.ds(0, NY - 1)], y_recv.at[k_mul])
            cols = pl.ds(pl.multiple_of(k_mul * width, width), width)

            def multiply(r, c):
                h = lax.div(r, 3)
                inner = pl.ds(pl.multiple_of(lax.rem(r, 3) * 256, 256), 256)
                acc[h, :, inner] += jnp.dot(
                    recvb[k_mul].reshape(SLOT_ROWS, width),
                    wbuf[h, cols, inner],
                    preferred_element_type=jnp.float32,
                )
                return c

            lax.fori_loop(0, 6, multiply, 0)

        return carry

    lax.fori_loop(0, CHUNKS + 4 + MULTIPLY_LAG, tick, 0)

    wait_bytes(wrecv.at[pl.ds(0, NY - 1)], w_sems.at[3])
    half = acc.shape[2] // 2

    def finish(h, part):
        rows = pl.ds(pl.multiple_of(part * COLUMN_ROWS, COLUMN_ROWS), COLUMN_ROWS)
        gate, lift = acc[h, rows, :half], acc[h, rows, half:]
        weight = wrecv[part].reshape(COLUMN_ROWS, 128)[:, :1].astype(jnp.float32)
        return rows, (weight * (gate / (1.0 + jnp.exp(-gate))) * lift).astype(jnp.bfloat16)

    def finish_other(part, c):
        rows, values = finish(1 - core, part)
        outsend[rows, :] = values
        return c

    def finish_own(part, c):
        rows, values = finish(core, part)
        out_ref[core, rows, :] = values
        return c

    lax.fori_loop(0, NY, finish_other, 0)
    out_copy = remote(outsend, out_ref.at[core], out_sems.at[0], out_sems.at[1], sibling)
    out_copy.start()
    lax.fori_loop(0, NY, finish_own, 0)

    def drain(k, c):
        wait_bytes(xall.at[k, pl.ds(0, NZ - 1)], z_send.at[k])
        wait_bytes(sendb.at[k, pl.ds(0, NX - 1)], x_send.at[k])
        wait_bytes(mid.at[k, pl.ds(0, NX - 1)], y_send.at[k])
        return c

    lax.fori_loop(0, CHUNKS, drain, 0)
    wait_bytes(weights.at[pl.ds(0, NZ - 1)], weight_send.at[0])
    wait_bytes(wsend.at[pl.ds(0, NX - 1)], w_sems.at[0])
    wait_bytes(wmid.at[pl.ds(0, NX - 1)], w_sems.at[2])
    other_copy.wait_send()
    out_copy.wait()


def dispatch(normed, weight, sel, gate_up):
    tokens, model = normed.shape
    width = model // CHUNKS
    inner = gate_up.shape[1]
    vmem, hbm = pl.BlockSpec(memory_space=pltpu.VMEM), pl.BlockSpec(memory_space=pl.ANY)
    dma = pltpu.SemaphoreType.DMA
    rows = (NX, NY, PEER_ROWS)
    return pl.pallas_call(
        dispatch_kernel,
        out_shape=jax.ShapeDtypeStruct((2, SLOT_ROWS, inner // 2), jnp.bfloat16),
        in_specs=[hbm, vmem, hbm, hbm],
        out_specs=vmem,
        scratch_shapes=[
            pltpu.VMEM(sel.shape, jnp.bfloat16),
            pltpu.VMEM((CHUNKS, NZ, tokens, width), jnp.bfloat16),
            pltpu.VMEM((NZ, tokens, 128), jnp.bfloat16),
            pltpu.VMEM((2, model, inner), jnp.bfloat16),
            pltpu.VMEM((CHUNKS, *rows, width), jnp.bfloat16),
            pltpu.VMEM((CHUNKS, *rows, width), jnp.bfloat16),
            pltpu.VMEM((CHUNKS, *rows, width), jnp.bfloat16),
            pltpu.VMEM((*rows, 128), jnp.bfloat16),
            pltpu.VMEM((*rows, 128), jnp.bfloat16),
            pltpu.VMEM((*rows, 128), jnp.bfloat16),
            pltpu.VMEM((2, SLOT_ROWS, inner), jnp.float32),
            pltpu.VMEM((SLOT_ROWS, inner // 2), jnp.bfloat16),
            dma((CHUNKS, 4)),
            dma((CHUNKS, 4)),
            dma((CHUNKS,)),
            dma((4,)),
            dma((4,)),
            dma((1,)),
            dma((CHUNKS,)),
            dma((CHUNKS,)),
            dma((CHUNKS,)),
            dma((CHUNKS,)),
            dma((4,)),
            dma((3,)),
            dma((2,)),
            dma((CHUNKS + 1,)),
        ],
        compiler_params=pltpu.CompilerParams(
            collective_id=1, has_side_effects=True, vmem_limit_bytes=62 * 1024 * 1024
        ),
        cost_estimate=pl.CostEstimate(
            flops=2 * SLOT_ROWS * model * (2 * inner + NZ * tokens),
            bytes_accessed=model * inner * 2,
            transcendentals=0,
        ),
        name="dispatch",
    )(normed, weight, sel, gate_up)


def attend_kernel(
    prompt_rows,
    q_hbm,
    kv_ref,
    prompt_ref,
    lengths_ref,
    w_hbm,
    hidden_hbm,
    gain_ref,
    router_hbm,
    routes_ref,
    resid_ref,
    normed_ref,
    weight_ref,
    sel_ref,
    q_ref,
    hidden_ref,
    router_ref,
    bias_ref,
    ranks,
    wc,
    pbuf,
    kvbuf,
    kcat,
    vcat,
    ctx,
    send_out,
    recv_out,
    load_sems,
    rank_sems,
    prompt_sems,
    kv_sems,
    z_recv,
    z_send,
    near_recv,
    spread_send,
    x_direct,
    x_relay,
    y_direct,
    y_relay,
    ctx_send,
    ctx_recv,
    out_send,
    out_recv,
):
    x, y, z, core = position()
    y_hi, y_lo = lax.div(y, 2), lax.rem(y, 2)
    z_pair, z_side = lax.div(z, 2), lax.rem(z, 2)
    xs = [lax.rem(x + d, NX) for d in range(NX)]
    ys = [lax.rem(y + d, NY) for d in range(NY)]
    x_dev = [device(xs[d], y, z, core) for d in range(NX)]
    y_dev = [device(x, ys[d], z, core) for d in range(NY)]
    z_dev = [device(x, y, lax.rem(z + d, NZ), core) for d in range(NZ)]
    sibling = device(x, y, z, 1 - core)
    twin = device(x, y, z_pair * 2 + 1 - z_side, core)
    cross = device(x, y, z_pair * 2 + 1 - z_side, 1 - core)
    pair_dev = device(x, y_hi * 2 + 1 - y_lo, z, core)

    barrier = pltpu.get_barrier_semaphore()
    partners = x_dev[1:] + y_dev[1:] + z_dev[1:] + [sibling, cross]
    for to in partners:
        pl.semaphore_signal(barrier, inc=1, device_id=to, device_id_type=MESH)

    steps = NZ // 2
    chunks = [lax.rem(z_pair + d, steps) for d in (0, 1, 3, 2)]

    def own_shard(half):
        return w_hbm.at[pl.ds(half * 256, 256)]

    def near(j, half, d, src):
        part = wc.at[j, y_lo, x, y_hi, half]
        to = (y_dev, x_dev)[half][d]
        remote(src, part, spread_send.at[j, 1], near_recv.at[j, half, d - 1], to).start()

    def xpart(j, d):
        return wc.at[j, :, xs[d], :, 0]

    def ypart(j, d):
        return wc.at[j, lax.rem(ys[d], 2), :, lax.div(ys[d], 2), 1]

    def xhalf(j, d, which):
        return wc.at[j, :, xs[d], which, 0]

    def yhalf(j, d, which):
        return wc.at[j, lax.rem(ys[d], 2), pl.ds(2 * which, 2), lax.div(ys[d], 2), 1]

    def begin(j):
        for d in (1, 3, 2):
            for half in range(2):
                near(j, half, d, wc.at[j, y_lo, x, y_hi, half])

    def spread(j):
        for half in range(2):
            for d in (1, 3, 2):
                if half == 0:
                    part = wc.at[j, lax.rem(ys[4 - d], 2), x, lax.div(ys[4 - d], 2), 0]
                else:
                    part = wc.at[j, y_lo, xs[4 - d], y_hi, 1]
                wait_bytes(part, near_recv.at[j, half, d - 1])
            parts, devs, sem = ((xpart, x_dev, x_direct), (ypart, y_dev, y_direct))[half]
            part = parts(j, 0)
            remote(part, part, spread_send.at[j, 0], sem.at[j, 0], devs[1]).start()
            remote(part, part, spread_send.at[j, 0], sem.at[j, 1], devs[3]).start()

    def relay(j):
        for parts, halves, devs, sem, next_sem in (
            (xpart, xhalf, x_dev, x_direct, x_relay),
            (ypart, yhalf, y_dev, y_direct, y_relay),
        ):
            wait_bytes(parts(j, 3), sem.at[j, 0])
            part = halves(j, 3, 0)
            remote(part, part, spread_send.at[j, 0], next_sem.at[j, 0], devs[1]).start()
            wait_bytes(parts(j, 1), sem.at[j, 1])
            part = halves(j, 1, 1)
            remote(part, part, spread_send.at[j, 0], next_sem.at[j, 1], devs[3]).start()

    def settle(j):
        for halves, next_sem in ((xhalf, x_relay), (yhalf, y_relay)):
            for which in range(2):
                wait_bytes(halves(j, 2, which), next_sem.at[j, which])

    tokens = kv_ref.shape[0]
    own_weight = [
        pltpu.make_async_copy(own_shard(half), wc.at[z_pair, y_lo, x, y_hi, half], load_sems.at[half])
        for half in range(2)
    ]
    for copy in own_weight:
        copy.start()
    spare = jnp.zeros((pbuf.shape[3] - prompt_rows, pbuf.shape[4]), jnp.float32)
    pbuf[core, y_lo, z] = jnp.concatenate([prompt_ref[...].astype(jnp.float32), spare], axis=0).astype(
        jnp.bfloat16
    )
    loads = [
        pltpu.make_async_copy(src, dst, load_sems.at[2 + i])
        for i, (src, dst) in enumerate(((q_hbm, q_ref), (hidden_hbm, hidden_ref), (router_hbm, router_ref)))
    ]
    for copy in loads:
        copy.start()
    kvbuf[core] = kv_ref[...]
    lane = lax.broadcasted_iota(jnp.int32, (tokens, 128), 1)
    row = lax.broadcasted_iota(jnp.int32, (tokens, 128), 0)
    named = routes_ref[0:1, :] == row
    for k in range(1, routes_ref.shape[0]):
        named = named | (routes_ref[k : k + 1, :] == row)
    earlier = jnp.where(row <= lane, 1.0, 0.0).astype(jnp.bfloat16)
    counted = jnp.dot(
        jnp.where(named, 1.0, 0.0).astype(jnp.bfloat16), earlier, preferred_element_type=jnp.float32
    )
    ranks[z] = jnp.where(named, counted, 0.0).astype(jnp.bfloat16)
    keys = bias_ref.shape[1]
    held = keys - 2 * tokens
    length = lengths_ref[0, z * 2 + y_lo]
    place = lax.broadcasted_iota(jnp.int32, (tokens, held), 1)
    bias_ref[:, :held] = jnp.where((place & 15) < prompt_rows, 0.0, neg_fill)
    place = lax.broadcasted_iota(jnp.int32, (tokens, 2 * tokens), 1)
    moment = lax.broadcasted_iota(jnp.int32, (tokens, 2 * tokens), 0) + core * tokens
    bias_ref[:, held:] = jnp.where((place <= moment) & (place < length), 0.0, neg_fill)

    pl.semaphore_wait(barrier, len(partners))
    for d in (1, 3, 2):
        for half in range(2):
            near(z_pair, half, d, own_shard(half))
    for d in (4, 3, 5, 2, 6, 1, 7):
        part = pbuf.at[core, y_lo, z]
        remote(part, part, prompt_sems.at[0], prompt_sems.at[5], z_dev[d]).start()
    for d in (1, 3, 2):
        for half in range(2):
            part = wc.at[z_pair, y_lo, x, y_hi, half]
            remote(own_shard(half), part, z_send.at[0], z_recv.at[half, d - 1], z_dev[2 * d]).start()
    kv_copy = remote(kv_ref, kvbuf.at[core], kv_sems.at[0], kv_sems.at[1], sibling)
    kv_copy.start()

    wait_bytes(pbuf.at[core, y_lo, pl.ds(0, NZ - 1)], prompt_sems.at[5])
    part = pbuf.at[core, y_lo]
    prompt_pair = remote(part, part, prompt_sems.at[1], prompt_sems.at[2], pair_dev)
    prompt_pair.start()
    for copy in own_weight:
        copy.wait()
    spread(chunks[0])

    for d in (4, 3, 5, 2, 6, 1, 7):
        remote(ranks.at[z], ranks.at[z], rank_sems.at[0], rank_sems.at[1], z_dev[d]).start()

    wait_bytes(pbuf.at[core, 1 - y_lo], prompt_sems.at[2])
    prompt_sib = remote(pbuf.at[core], pbuf.at[core], prompt_sems.at[3], prompt_sems.at[4], sibling)
    prompt_sib.start()
    for d, j in ((1, chunks[2]), (3, chunks[1]), (2, chunks[3])):
        for half in range(2):
            wait_bytes(wc.at[j, y_lo, x, y_hi, half], z_recv.at[half, d - 1])
        begin(j)
    wait_bytes(kvbuf.at[1 - core], kv_sems.at[1])
    wait_bytes(pbuf.at[1 - core], prompt_sems.at[4])
    prompt_keys = pbuf[...].reshape(-1, pbuf.shape[-1])
    own_rows = kvbuf[...].reshape(2 * tokens, kvbuf.shape[-1])
    for g in range(KEY_VALUE_HEADS):
        low, high = g * HEAD_SIZE, (KEY_VALUE_HEADS + g) * HEAD_SIZE
        kcat[g, :held, :] = prompt_keys[:, low : low + HEAD_SIZE]
        kcat[g, held:, :] = own_rows[:, low : low + HEAD_SIZE]
        vcat[g, :held, :] = prompt_keys[:, high : high + HEAD_SIZE]
        vcat[g, held:, :] = own_rows[:, high : high + HEAD_SIZE]
    loads[0].wait()

    pairs = QUERY_HEADS // 2
    sections = ctx.shape[2]

    def attend(section, i, carry):
        g = section * KEY_VALUE_HEADS // sections
        j = section * (pairs // sections) + i
        query = jnp.concatenate(
            [
                q_ref[:, pl.ds(pl.multiple_of((j * 2 + n) * HEAD_SIZE, HEAD_SIZE), HEAD_SIZE)]
                for n in range(2)
            ],
            axis=0,
        )
        scores = lax.dot_general(
            query, kcat[g], (((1,), (1,)), ((), ())), preferred_element_type=jnp.float32
        )
        scores = scores * (HEAD_SIZE**-0.5) + jnp.concatenate([bias_ref[...], bias_ref[...]], axis=0)
        raised = jnp.exp(scores - jnp.max(scores, axis=1, keepdims=True))
        denom = jnp.sum(raised, axis=1, keepdims=True)
        mixed = jnp.dot(raised.astype(jnp.bfloat16), vcat[g], preferred_element_type=jnp.float32)
        mixed = (mixed / denom).astype(jnp.bfloat16)
        for n in range(2):
            cols = pl.ds(pl.multiple_of((i * 2 + n) * HEAD_SIZE, HEAD_SIZE), HEAD_SIZE)
            ctx[z_side, core, section, :, cols] = mixed[n * tokens : (n + 1) * tokens]
        return carry

    def ctx_move(section, side, to, which):
        part = ctx.at[side, core, section]
        return remote(part, part, ctx_send.at[section, which], ctx_recv.at[section, which], to)

    for section in range(sections):
        lax.fori_loop(0, pairs // sections, functools.partial(attend, section), 0)
        ctx_move(section, z_side, twin, 0).start()
        ctx_move(section, z_side, sibling, 1).start()
        if section == 0:
            spread(chunks[2])
            relay(chunks[0])
            spread(chunks[1])
    relay(chunks[2])
    spread(chunks[3])
    relay(chunks[1])

    relay(chunks[3])
    for section in range(sections):
        wait_bytes(ctx.at[1 - z_side, core, section], ctx_recv.at[section, 0])
        ctx_move(section, 1 - z_side, sibling, 2).start()
    for section in range(sections):
        wait_bytes(ctx.at[z_side, 1 - core, section], ctx_recv.at[section, 1])
        wait_bytes(ctx.at[1 - z_side, 1 - core, section], ctx_recv.at[section, 2])

    def out_move(j, side, who, to, which):
        return remote(
            send_out.at[j, side, who],
            recv_out.at[z_side, core, j],
            out_send.at[j, which],
            out_recv.at[j, which],
            to,
        )

    def out_moves(j):
        return (
            out_move(j, 1 - z_side, core, twin, 0),
            out_move(j, 1 - z_side, 1 - core, cross, 1),
            out_move(j, z_side, 1 - core, sibling, 2),
        )

    deep = 4096 // NX

    def project(j):
        settle(j)

        def part(i, total):
            cols = pl.ds(pl.multiple_of(lax.rem(i, 2) * deep, deep), deep)
            left = ctx[:, :, lax.div(i, 2), :, cols].reshape(4 * tokens, deep)
            right = jnp.concatenate(
                [wc[j, 0, i].reshape(deep, 128), wc[j, 1, i].reshape(deep, 128)], axis=1
            )
            return total + jnp.dot(left, right, preferred_element_type=jnp.float32)

        total = lax.fori_loop(0, NX, part, jnp.zeros((4 * tokens, 256), jnp.float32))
        send_out[j] = total.astype(jnp.bfloat16).reshape(2, 2, tokens, 256)
        for move in out_moves(j):
            move.start()
        recv_out[z_side, core, j] = send_out[j, z_side, core]

    def chunk_at(i):
        d = jnp.where(i == 1, 3, jnp.where(i == 2, 1, jnp.where(i == 3, 2, 0)))
        return lax.rem(z_pair + d, steps)

    def project_at(i, carry):
        project(chunk_at(i))
        return carry

    def add_up(i, square):
        j = chunk_at(i)
        wait_bytes(recv_out.at[1 - z_side, core, j], out_recv.at[j, 0])
        wait_bytes(recv_out.at[1 - z_side, 1 - core, j], out_recv.at[j, 1])
        wait_bytes(recv_out.at[z_side, 1 - core, j], out_recv.at[j, 2])
        for side in range(2):
            for lo in range(2):
                for who in range(2):
                    cols = pl.ds(pl.multiple_of((((j * 2 + side) * 2 + lo) * 2 + who) * 128, 128), 128)
                    part = recv_out[side, who, j, :, lo * 128 : (lo + 1) * 128].astype(jnp.float32)
                    rounded = (hidden_ref[:, cols].astype(jnp.float32) + part).astype(jnp.bfloat16)
                    resid_ref[:, cols] = rounded
                    wide = rounded.astype(jnp.float32)
                    square = square + wide * wide
        return square

    lax.fori_loop(0, steps, project_at, 0)

    wait_bytes(ranks.at[pl.ds(0, NZ - 1)], rank_sems.at[1])
    chosen, source, slot = plane_expert(SLOT_ROWS, z)
    picker = jnp.where(chosen, 1.0, 0.0).astype(jnp.bfloat16)
    for b in range(NZ):
        found = jnp.dot(picker, ranks[b], preferred_element_type=jnp.float32)
        hit = (found == slot + 1.0) & (source == float(b))
        sel_ref[:, b * tokens : (b + 1) * tokens] = jnp.where(hit, 1.0, 0.0).astype(jnp.bfloat16)

    loads[1].wait()
    loads[2].wait()
    square = lax.fori_loop(0, steps, add_up, jnp.zeros((tokens, 128), jnp.float32))
    model = hidden_ref.shape[1]
    scale = lax.rsqrt(jnp.sum(square, axis=1, keepdims=True) * (1.0 / model) + eps_norm)

    def normalise(i, logits):
        cols = pl.ds(pl.multiple_of(i * 512, 512), 512)
        part = (resid_ref[:, cols].astype(jnp.float32) * scale * gain_ref[:, cols]).astype(jnp.bfloat16)
        normed_ref[:, cols] = part
        return logits + jnp.dot(part, router_ref[cols, :], preferred_element_type=jnp.float32)

    logits = lax.fori_loop(0, model // 512, normalise, jnp.zeros((tokens, 128), jnp.float32))
    named = ranks[z].astype(jnp.float32).T > 0.0
    masked = jnp.where(named, logits, neg_fill)
    raised = jnp.where(named, jnp.exp(masked - jnp.max(masked, axis=1, keepdims=True)), 0.0)
    weight_ref[...] = (raised / jnp.sum(raised, axis=1, keepdims=True)).astype(jnp.bfloat16)

    kv_copy.wait_send()
    wait_bytes(ranks.at[pl.ds(0, NZ - 1)], rank_sems.at[0])
    wait_bytes(pbuf.at[0, 0, pl.ds(0, NZ - 1)], prompt_sems.at[0])
    prompt_pair.wait_send()
    prompt_sib.wait_send()
    wait_bytes(wc.at[0, 0, pl.ds(0, 3), :, 0], z_send.at[0])
    for section in range(sections):
        for which in range(3):
            wait_bytes(ctx.at[z_side, core, section], ctx_send.at[section, which])

    def drain(j, carry):
        wait_bytes(wc.at[j, :, pl.ds(0, 3)], spread_send.at[j, 0])
        wait_bytes(wc.at[j, 0, pl.ds(0, 3), :, 0], spread_send.at[j, 1])
        for move in out_moves(j):
            move.wait_send()
        return carry

    lax.fori_loop(0, steps, drain, 0)


def attend_all(queries, key_value, prompt, lengths, out_weight, hidden, gain, router, routes):
    tokens, model = queries.shape
    vmem, hbm = pl.BlockSpec(memory_space=pltpu.VMEM), pl.BlockSpec(memory_space=pl.ANY)
    smem = pl.BlockSpec(memory_space=pltpu.SMEM)
    dma = pltpu.SemaphoreType.DMA
    kv_width = key_value.shape[1]
    prompt_rows = prompt.shape[0]
    held_rows = -(-prompt_rows // 16) * 16
    keys = 2 * NYL * NZ * held_rows + 2 * tokens
    experts = router.shape[1]
    return pl.pallas_call(
        functools.partial(attend_kernel, prompt_rows),
        out_shape=(
            jax.ShapeDtypeStruct((tokens, model), jnp.bfloat16),
            jax.ShapeDtypeStruct((tokens, model), jnp.bfloat16),
            jax.ShapeDtypeStruct((tokens, experts), jnp.bfloat16),
            jax.ShapeDtypeStruct((SLOT_ROWS, NZ * tokens), jnp.bfloat16),
        ),
        in_specs=[hbm, vmem, vmem, smem, hbm, hbm, vmem, hbm, vmem],
        out_specs=[vmem] * 4,
        scratch_shapes=[
            pltpu.VMEM((tokens, model), jnp.bfloat16),
            pltpu.VMEM((tokens, model), jnp.bfloat16),
            pltpu.VMEM((model, experts), jnp.bfloat16),
            pltpu.VMEM((tokens, keys), jnp.float32),
            pltpu.VMEM((NZ, tokens, experts), jnp.bfloat16),
            pltpu.VMEM((NZ // 2, 2, NX, 2, 2, 256, 128), jnp.bfloat16),
            pltpu.VMEM((2, 2, NZ, held_rows, kv_width), jnp.bfloat16),
            pltpu.VMEM((2, tokens, kv_width), jnp.bfloat16),
            pltpu.VMEM((KEY_VALUE_HEADS, keys, HEAD_SIZE), jnp.bfloat16),
            pltpu.VMEM((KEY_VALUE_HEADS, keys, HEAD_SIZE), jnp.bfloat16),
            pltpu.VMEM((2, 2, 2, tokens, model // 2), jnp.bfloat16),
            pltpu.VMEM((NZ // 2, 2, 2, tokens, 256), jnp.bfloat16),
            pltpu.VMEM((2, 2, NZ // 2, tokens, 256), jnp.bfloat16),
            dma((5,)),
            dma((2,)),
            dma((6,)),
            dma((2,)),
            dma((2, 3)),
            dma((1,)),
            dma((NZ // 2, 2, 3)),
            dma((NZ // 2, 2)),
            dma((NZ // 2, 2)),
            dma((NZ // 2, 2)),
            dma((NZ // 2, 2)),
            dma((NZ // 2, 2)),
            dma((2, 3)),
            dma((2, 3)),
            dma((NZ // 2, 3)),
            dma((NZ // 2, 3)),
        ],
        compiler_params=pltpu.CompilerParams(
            collective_id=2, has_side_effects=True, vmem_limit_bytes=62 * 1024 * 1024
        ),
        cost_estimate=pl.CostEstimate(
            flops=2 * tokens * model * (model + 2 * keys), bytes_accessed=8 * tokens * model, transcendentals=0
        ),
        name="attend",
    )(queries, key_value, prompt, lengths, out_weight, hidden, gain, router, routes)


def local(
    hidden,
    queries,
    response_key_value,
    prompt_kv,
    lengths,
    out_weight,
    norm_gain,
    router,
    gate_up,
    routes,
):
    resid_out, normed, weight, sel = attend_all(
        queries[0],
        response_key_value[0],
        prompt_kv[0],
        lengths,
        out_weight,
        hidden[0],
        norm_gain[None, :],
        router,
        routes[0].T,
    )
    slots = dispatch(normed, weight, sel, gate_up[0])
    expert_act = (
        slots.reshape(2, 2, 2, NX, NZ, CAP, -1)
        .transpose(3, 1, 4, 2, 0, 5, 6)
        .reshape(1, 2 * NX * NZ * NY, CAP, -1)
    )
    return (resid_out[None], expert_act)


def solution(mesh):
    placed = (
        P("grp", "exp", None),
        P("grp", "exp", None),
        P("grp", "exp", None),
        P("grp", "exp", None),
        P("grp", None),
        P("grp", "exp"),
        P(),
        P(),
        P(("grp", "exp"), None, None),
        P("grp", "exp", None),
    )
    return jax.shard_map(
        local,
        mesh=mesh,
        in_specs=placed,
        out_specs=(P("grp", "exp", None), P(("grp", "exp"), None, None, None)),
        check_vma=False,
    )
```
